32 devices in a mesh: dp: 2 (over core), tensor: 2 (over x), expert: 8 (over z, y).
Axes of the slice: x: 2, y: 2, z: 4, core: 2. Of those that a mesh axis runs over, the one named last changes fastest.
Arguments:
- checkpoint: bfloat16 [2048, 2048], P(('dp', 'expert'), 'tensor'), may hold values from -6 to 6
- scales: float32 [2048], P(('dp', 'expert')), may hold values from 0.5 to 2
- out_grad: bfloat16 [2048, 2048], P(('dp', 'expert'), 'tensor'), may hold values from -1.5 to 1.5
- expert_ids: int32 [2048, 8], P(('dp', 'expert')), may hold values from 0 to 15, all different within a row; in each aligned block of 128 rows (0 to 127, 128 to 255, ...) at most 64 rows name the same one
- gates: float32 [2048, 8], P(('dp', 'expert')), may hold values from 0.05 to 1
- w_gate: bfloat16 [16, 768, 2048], P(('dp', 'expert'), 'tensor'), may hold values from -0.125 to 0.125
- w_up: bfloat16 [16, 768, 2048], P(('dp', 'expert'), 'tensor'), may hold values from -0.125 to 0.125
- w_down: bfloat16 [16, 768, 2048], P(('dp', 'expert'), 'tensor'), may hold values from -0.21875 to 0.21875
Outputs:
- grad_input: bfloat16 [2048, 2048], P(('dp', 'expert'), 'tensor')
- grad_gates: float32 [2048, 8], P(('dp', 'expert'))
The draws below stay inside these ranges and needn't reach their ends.
Inputs may be any that keep to these rules, and one draw needn't show every extreme that they name: `expert_ids`: each row names 8 different experts. Among the 128 rows of one device (aligned blocks of rows), no expert is named more than 64 times, a bound that some block reaches.
All inputs are finite; a program needn't handle non-finite values.
Results may differ from the reference program's by a relative error of at most 0.012.
Values may be sent and summed in bfloat16 or wider, within the bound.
No kernel may reach another device: no remote copies, remote signals or barrier semaphores. Data moves between devices by JAX's collectives and lax.ppermute only.
A program may use at most 64 MiB of HBM per device.

```python
import math
import jax
import jax.numpy as jnp
import numpy as np
from jax import lax

D = 2048
FF = 768
TOP = 8
TOK_DEV = 128
EXPERTS = 16
CAP = 64
TOKENS = 2048
N_TENSOR = 2


def block_levels(rng, dims, cuts, smallest, high):
    factor_of, own = 1.0, jax.random.fold_in(rng, 6)
    for axis_at, parts in cuts:
        draws = jnp.exp(jax.random.uniform(jax.random.fold_in(own, axis_at), (parts,), jnp.float32, smallest / len(cuts), high / len(cuts)))
        factor_of = factor_of * jnp.repeat(draws, dims[axis_at] // parts).reshape([-1 if axis == axis_at else 1 for axis in range(len(dims))])
    return factor_of


def deal_out(own_key, own, number, rows, count, top, most, lean):
    order = jax.random.permutation(own_key, count)
    heavy_load, usual = portions_of(count, rows * top, most, lean, True), portions_of(count, rows * top, most, lean, False)
    places = jnp.arange(count)

    def named(sizes, turn):
        used = int((sizes > 0).sum())
        fixed = max(1, used // 4)
        passed = fixed + (places - fixed + turn * (used - fixed)) % max(1, count - fixed)
        return jnp.zeros((count,), jnp.int32).at[order[jnp.where(places < fixed, places, passed)]].set(jnp.asarray(sizes, jnp.int32))

    sizes = jnp.where(number % 4 == 0, named(heavy_load, number // 4), named(usual, number - number // 4 - 1))
    mixed = jax.random.permutation(jax.random.fold_in(own, 3), count)
    source_of, taker = mixed[0:count // 2 * 2:2], mixed[1:count // 2 * 2:2]
    room = jnp.minimum(sizes[source_of] - 1, most - sizes[taker]) // 2
    room = jnp.where((source_of == order[0]) | (taker == order[0]) | (sizes[taker] == 0), 0, jnp.maximum(room, 0))
    passed = jax.random.randint(jax.random.fold_in(own, 4), (count // 2,), 0, 1 << 20) % (room + 1)
    sizes = sizes.at[source_of].add(-passed).at[taker].add(passed)
    labels = jnp.searchsorted(jnp.cumsum(sizes), jnp.arange(rows * top), side="right").astype(jnp.int32)
    table = labels.reshape(top, rows).T
    table = table[jax.random.permutation(jax.random.fold_in(own, 1), rows)]
    turn = jax.random.randint(jax.random.fold_in(own, 2), (rows, 1), 0, top)
    return jnp.take_along_axis(table, (jnp.arange(top)[None, :] + turn) % top, axis=1)


def portions_of(number_of, total, limit, slope, full):
    loads = [(1 << 20) // math.isqrt(rank ** slope) + 1 for rank in range(1, number_of + 1)]
    largest = limit if full else min(limit, max(-(-total // number_of), total * loads[0] // sum(loads)))
    least = 1 if total - largest >= number_of - 1 else 0
    holding, surplus = [largest] + [least] * (number_of - 1), total - largest - least * (number_of - 1)
    while surplus > 0:
        movable = [i for i in range(1, number_of) if holding[i] < largest] or [i for i in range(1, number_of) if holding[i] < limit]
        whole, budget = sum([loads[i] for i in movable]), surplus
        for i in movable:
            extra = min(limit - holding[i], max(1, budget * loads[i] // whole), surplus)
            holding[i] = holding[i] + extra
            surplus = surplus - extra
    return np.array(holding)


def noise(rng, shape, width, most, shards=(), kind=jnp.bfloat16):
    gain = block_levels(rng, shape, shards, -0.22, 0.18) if shards else 1.0
    drawn = jax.random.normal(rng, shape, jnp.float32) * width * gain
    return jnp.minimum(jnp.maximum(drawn, -most), most).astype(kind)


def setup_inputs(seed: int = 0) -> dict:
    seeds = jax.random.split(jax.random.key(seed), 9)
    checkpoint = noise(seeds[0], (TOKENS, D), 1.0, 6.0, ((0, 16), (1, 2)))
    scales = jnp.clip(jnp.exp(math.log(2.0) - 1.3862944 * jax.random.uniform(seeds[1], (TOKENS,), jnp.float32) ** block_levels(seeds[1], (TOKENS,), ((0, 16),), -0.2, 0.2)), 0.5, 2.0)
    out_grad = noise(seeds[2], (TOKENS, D), 0.25, 1.5, ((0, 16), (1, 2)))
    expert_ids_keys = jax.random.split(jax.random.fold_in(seeds[3], 1), TOKENS // TOK_DEV)
    expert_ids_turns = jax.random.permutation(jax.random.fold_in(seeds[3], 3), TOKENS // TOK_DEV)
    expert_ids = jax.vmap(lambda own, number: deal_out(jax.random.fold_in(seeds[3], 2), own, number, TOK_DEV, EXPERTS, TOP, CAP, 0))(expert_ids_keys, expert_ids_turns).reshape((TOKENS, TOP))
    gates = jnp.clip(jnp.exp(math.log(1.0) - 2.9957323 * jax.random.uniform(seeds[4], (TOKENS, TOP), jnp.float32) ** block_levels(seeds[4], (TOKENS, TOP), ((0, 16),), -0.2, 0.2)), 0.05, 1.0)
    w_gate = noise(seeds[5], (EXPERTS, FF, D), D ** -0.5, 0.125, ((0, 16), (1, 2)))
    w_up = noise(seeds[6], (EXPERTS, FF, D), D ** -0.5, 0.125, ((0, 16), (1, 2)))
    w_down = noise(seeds[7], (EXPERTS, FF, D), FF ** -0.5, 0.21875, ((0, 16), (1, 2)))
    return {"checkpoint": checkpoint, "scales": scales, "out_grad": out_grad, "expert_ids": expert_ids, "gates": gates, "w_gate": w_gate, "w_up": w_up, "w_down": w_down}


def silu_parts(gate_pre, up_pre, back):
    sigma = jax.nn.sigmoid(gate_pre)
    swish = gate_pre * sigma
    hidden = (swish * up_pre).astype(jnp.bfloat16)
    d_gate = (back * up_pre * sigma * (1.0 + gate_pre * (1.0 - sigma))).astype(jnp.bfloat16)
    d_up = (back * swish).astype(jnp.bfloat16)
    return hidden, d_gate, d_up


def reference(checkpoint, scales, out_grad, expert_ids, gates, w_gate, w_up, w_down):
    dequant = (checkpoint.astype(jnp.float32) * scales[:, None]).astype(jnp.bfloat16)
    blocks = TOKENS // TOK_DEV
    pair_count = TOK_DEV * TOP
    block_ids = expert_ids.reshape(blocks, pair_count).astype(jnp.int32)
    onehot = (block_ids[:, :, None] == jnp.arange(EXPERTS, dtype=jnp.int32)[None, None, :]).astype(jnp.int32)
    earlier = jnp.cumsum(onehot, axis=1) - onehot
    position = jnp.sum(earlier * onehot, axis=2).astype(jnp.int32)
    column = jnp.arange(blocks, dtype=jnp.int32)[:, None] * CAP + position
    pair_index = jnp.arange(blocks * pair_count, dtype=jnp.int32).reshape(blocks, pair_count)
    table = jnp.full((EXPERTS, blocks * CAP), TOKENS * TOP, jnp.int32)
    table = table.at[block_ids.reshape(-1), column.reshape(-1)].set(pair_index.reshape(-1))
    gate_flat = gates.reshape(-1)
    quarter = FF // N_TENSOR
    slot_total = blocks * CAP
    contract = (((1,), (1,)), ((), ()))

    def per_expert(carry, inputs):
        grad_sum, gate_sum = carry
        pairs, weight_gate, weight_up, weight_down = inputs
        token_of = (pairs // TOP).astype(jnp.int32)
        rows_in = jnp.take(dequant, token_of, axis=0, mode="fill", fill_value=0)
        grads_in = jnp.take(out_grad, token_of, axis=0, mode="fill", fill_value=0)
        gate_pre = lax.dot_general(rows_in, weight_gate, contract, preferred_element_type=jnp.float32)
        up_pre = lax.dot_general(rows_in, weight_up, contract, preferred_element_type=jnp.float32)
        back = lax.dot_general(grads_in, weight_down, contract, preferred_element_type=jnp.float32)
        hidden, d_gate, d_up = silu_parts(gate_pre, up_pre, back)
        product = hidden.astype(jnp.float32) * back
        contrib = jnp.zeros((slot_total, D), jnp.float32)
        gate_term = jnp.zeros((slot_total,), jnp.float32)
        for rank in range(N_TENSOR):
            low = rank * quarter
            high = low + quarter
            part_sum = jnp.sum(product[:, low:high], axis=1).astype(jnp.bfloat16)
            gate_term = gate_term + lax.optimization_barrier(part_sum).astype(jnp.float32)
            piece = jnp.dot(d_gate[:, low:high], weight_gate[low:high, :], preferred_element_type=jnp.float32)
            piece = piece + jnp.dot(d_up[:, low:high], weight_up[low:high, :], preferred_element_type=jnp.float32)
            contrib = contrib + lax.optimization_barrier(piece.astype(jnp.bfloat16)).astype(jnp.float32)
        summed = lax.optimization_barrier(contrib.astype(jnp.bfloat16)).astype(jnp.float32)
        weight = jnp.take(gate_flat, pairs, mode="fill", fill_value=0)
        grad_sum = grad_sum.at[token_of].add(weight[:, None] * summed, mode="drop")
        gate_sum = gate_sum.at[pairs].add(gate_term, mode="drop")
        return (grad_sum, gate_sum), None

    start = (jnp.zeros((TOKENS, D), jnp.float32), jnp.zeros((TOKENS * TOP,), jnp.float32))
    (grad_sum, gate_sum), _ = lax.scan(per_expert, start, (table, w_gate, w_up, w_down))
    return grad_sum.astype(jnp.bfloat16), gate_sum.reshape(TOKENS, TOP)
```

```python
import functools
import jax
import jax.numpy as jnp
from jax import lax
from jax.experimental import pallas as pl
from jax.experimental.pallas import tpu as pltpu
from jax.sharding import PartitionSpec as P


def slot_table(expert_ids, expert_count, slot_cap):
    token_rows = expert_ids.shape[0]
    pick_count = expert_ids.shape[1]
    chosen = expert_ids.reshape(-1)
    onehot = (chosen[:, None] == jnp.arange(expert_count, dtype=jnp.int32)[None, :]).astype(
        jnp.int32
    )
    earlier = jnp.cumsum(onehot, axis=0) - onehot
    position = jnp.sum(earlier * onehot, axis=1)
    slot_of = chosen * slot_cap + position
    token_ids = jnp.arange(token_rows * pick_count, dtype=jnp.int32) // pick_count
    owner = jnp.full((expert_count * slot_cap,), token_rows, jnp.int32).at[slot_of].set(token_ids)
    return (slot_of, owner)


def finish(gate_pre, up_pre, back, weight_gate, weight_up):
    sigma = jax.nn.sigmoid(gate_pre)
    swish = gate_pre * sigma
    hidden = (swish * up_pre).astype(jnp.bfloat16)
    gate_part = jnp.sum(hidden.astype(jnp.float32) * back, axis=1).astype(jnp.bfloat16)
    d_gate = (back * up_pre * sigma * (1.0 + gate_pre * (1.0 - sigma))).astype(jnp.bfloat16)
    d_up = (back * swish).astype(jnp.bfloat16)
    input_part = jnp.dot(d_gate, weight_gate, preferred_element_type=jnp.float32)
    input_part = input_part + jnp.dot(d_up, weight_up, preferred_element_type=jnp.float32)
    return (input_part.astype(jnp.bfloat16), gate_part)


def close_expert(input_part, gate_part, sources, items, model_width):
    shaped = input_part.reshape(sources, items, model_width)
    gate_shaped = gate_part.reshape(sources, items)
    summed = lax.psum_scatter(
        shaped.astype(jnp.float32).astype(jnp.bfloat16), "tensor", scatter_dimension=2, tiled=True
    )
    return (summed, gate_shaped)


def body_routed(checkpoint, scales, out_grad, expert_ids, gates, w_gate, w_up, w_down):
    expert_count = lax.axis_size("dp") * lax.axis_size("expert")
    token_rows = checkpoint.shape[0]
    pick_count = expert_ids.shape[1]
    slot_cap = min(token_rows, token_rows * pick_count // expert_count)
    weight_gate = w_gate[0]
    weight_up = w_up[0]
    weight_down = w_down[0]
    model_width = weight_gate.shape[1]
    contract = (((1,), (1,)), ((), ()))
    dequant = (checkpoint.astype(jnp.float32) * scales[:, None]).astype(jnp.bfloat16)
    slot_of, owner = slot_table(expert_ids, expert_count, slot_cap)
    full_x, full_grad = (
        lax.all_gather(dequant, "tensor", axis=1, tiled=True),
        lax.all_gather(out_grad, "tensor", axis=1, tiled=True),
    )
    send_x = jnp.take(full_x, owner, axis=0, mode="fill", fill_value=0).reshape(
        expert_count, slot_cap, model_width
    )
    send_grad = jnp.take(full_grad, owner, axis=0, mode="fill", fill_value=0).reshape(
        expert_count, slot_cap, model_width
    )
    rows_in = lax.all_to_all(send_x, ("dp", "expert"), split_axis=0, concat_axis=0, tiled=True)
    grads_in = lax.all_to_all(send_grad, ("dp", "expert"), split_axis=0, concat_axis=0, tiled=True)
    sources, items, width = rows_in.shape
    rows_flat = rows_in.reshape(sources * items, width)
    grads_flat = grads_in.reshape(sources * items, width)
    gate_pre = lax.dot_general(rows_flat, weight_gate, contract, preferred_element_type=jnp.float32)
    up_pre = lax.dot_general(rows_flat, weight_up, contract, preferred_element_type=jnp.float32)
    back = lax.dot_general(grads_flat, weight_down, contract, preferred_element_type=jnp.float32)
    input_part, gate_part = finish(gate_pre, up_pre, back, weight_gate, weight_up)
    input_part, gate_part = close_expert(input_part, gate_part, sources, items, model_width)
    back_input, back_gate = (
        lax.all_to_all(input_part, ("dp", "expert"), split_axis=0, concat_axis=0, tiled=True),
        lax.all_to_all(gate_part, ("dp", "expert"), split_axis=0, concat_axis=0, tiled=True),
    )
    share_width = back_input.shape[2]
    picked = jnp.take(back_input.reshape(expert_count * slot_cap, share_width), slot_of, axis=0)
    picked = picked.astype(jnp.float32).reshape(token_rows, pick_count, share_width)
    weighted = jnp.sum(picked * gates[:, :, None], axis=1)
    gate_pairs = (
        jnp.take(back_gate.reshape(-1), slot_of, axis=0)
        .astype(jnp.float32)
        .reshape(token_rows, pick_count)
    )
    gate_out = lax.psum(gate_pairs.astype(jnp.bfloat16), "tensor").astype(jnp.float32)
    return (weighted.astype(jnp.bfloat16), gate_out)


def pack_picks(expert_ids, gates, width):
    high = gates.astype(jnp.bfloat16)
    low = (gates - high.astype(jnp.float32)).astype(jnp.bfloat16)
    parts = [expert_ids.astype(jnp.bfloat16), high, low]
    flat = jnp.concatenate([part.T.reshape(-1) for part in parts])
    rows = -(-flat.shape[0] // (16 * width)) * 16
    return jnp.pad(flat, (0, rows * width - flat.shape[0])).reshape(rows, width)


def expert_kernel(tops, way, info_ref, u_ref, v_ref, m_ref, n_ref, wg_ref, wu_ref, wd_ref, *outs):
    f32 = jnp.float32
    contract = (((1,), (1,)), ((), ()))
    _, token_rows, width = m_ref.shape
    rows = 2 * token_rows
    half = token_rows // 2
    units = wg_ref.shape[0] // 2
    mine = pl.ds(pl.multiple_of(info_ref[0] * width, width), width)
    other = pl.ds(pl.multiple_of((1 - info_ref[0]) * width, width), width)

    def project(first, second, w_ref):
        low = lax.dot_general(first, w_ref[:, mine], contract, preferred_element_type=f32)
        return low + lax.dot_general(second, w_ref[:, other], contract, preferred_element_type=f32)

    def weight_of(ref, expert):
        pick_rows = ref[rows:]

        def segment(kind, k):
            at = (kind * tops + k) * token_rows
            row, col = at // width, at % width
            return pick_rows[row : row + 1, col : col + token_rows].astype(f32)

        total = jnp.zeros((1, token_rows), f32)
        for k in range(tops):
            chosen = segment(0, k) == expert.astype(f32)
            total = total + jnp.where(chosen, segment(1, k) + segment(2, k), 0.0)
        return jnp.broadcast_to(total, (128, token_rows)).T[:, :1]

    x_mine = jnp.concatenate([u_ref[:token_rows], v_ref[:token_rows]], axis=0)
    x_other = jnp.concatenate([u_ref[token_rows:rows], v_ref[token_rows:rows]], axis=0)
    gate_pre = project(x_mine, x_other, wg_ref)
    up_pre = project(x_mine, x_other, wu_ref)
    back = project(m_ref[...].reshape(rows, width), n_ref[...].reshape(rows, width), wd_ref)
    sigma = jax.nn.sigmoid(gate_pre)
    swish = gate_pre * sigma
    hidden = (swish * up_pre).astype(jnp.bfloat16)
    product = hidden.astype(f32) * back
    weights = []
    for which in range(2):
        expert = info_ref[1 + which]
        weights.append(jnp.concatenate([weight_of(u_ref, expert), weight_of(v_ref, expert)], axis=0))
        term = jnp.sum(product[:, which * units : (which + 1) * units], axis=1, keepdims=True)
        term = term.astype(jnp.bfloat16).astype(f32)
        outs[-1][which] = jnp.broadcast_to(term, (rows, 128)).T[:8]
    lane = lax.broadcasted_iota(jnp.int32, back.shape, 1)
    scaled = back * jnp.where(lane < units, weights[0], weights[1])
    d_gate = (scaled * up_pre * sigma * (1.0 + gate_pre * (1.0 - sigma))).astype(jnp.bfloat16)
    d_up = (scaled * swish).astype(jnp.bfloat16)

    def spread(cols):
        piece = jnp.dot(d_gate, wg_ref[:, cols], preferred_element_type=f32)
        piece = piece + jnp.dot(d_up, wu_ref[:, cols], preferred_element_type=f32)
        return piece.astype(jnp.bfloat16)

    far, near = spread(other), spread(mine)
    if way == "x":
        send, keep = outs[:2]
        send[...], keep[...] = far.reshape(2, token_rows, width), near.reshape(2, token_rows, width)
    elif way == "y":
        send, keep = outs[:2]
        keep[0], send[0] = near[:token_rows], near[token_rows:]
        keep[1], send[1] = far[:token_rows], far[token_rows:]
    else:
        a_send, a_keep, b_send, b_keep = outs[:4]
        a_send[0], a_send[1] = far[:half], far[token_rows : token_rows + half]
        b_keep[1], b_send[1] = far[half:token_rows], far[token_rows + half :]
        a_keep[0], a_keep[1] = near[:half], near[token_rows : token_rows + half]
        b_keep[0], b_send[0] = near[half:token_rows], near[token_rows + half :]


def run_expert(tops, way, info, u, v, m, n, wg, wu, wd):
    _, token_rows, width = m.shape
    hidden, model_width = wg.shape
    rows = 2 * token_rows
    vmem = pl.BlockSpec(memory_space=pltpu.VMEM)
    count, part = (4, token_rows // 2) if way == "both" else (2, token_rows)
    share = jax.ShapeDtypeStruct((2, part, width), jnp.bfloat16)
    return pl.pallas_call(
        functools.partial(expert_kernel, tops, way),
        in_specs=[pl.BlockSpec(memory_space=pltpu.SMEM)] + [vmem] * 7,
        out_specs=[vmem] * (count + 1),
        out_shape=[share] * count + [jax.ShapeDtypeStruct((2, 8, rows), jnp.float32)],
        compiler_params=pltpu.CompilerParams(vmem_limit_bytes=32 * 1024 * 1024),
        cost_estimate=pl.CostEstimate(
            flops=10 * rows * hidden * model_width,
            bytes_accessed=6 * rows * model_width + 6 * hidden * model_width,
            transcendentals=rows * hidden,
        ),
    )(info, u, v, m, n, wg, wu, wd)


def add(left, right):
    return (left.astype(jnp.float32) + right.astype(jnp.float32)).astype(jnp.bfloat16)


def body_dense(checkpoint, scales, out_grad, expert_ids, gates, w_gate, w_up, w_down):
    experts = lax.axis_size("expert")
    ring = experts // 2
    core = lax.axis_index("dp")
    place = lax.axis_index("expert")
    slow, fast = place // 2, place % 2
    side = lax.axis_index("tensor")
    token_rows, width = checkpoint.shape
    tops = expert_ids.shape[1]

    def over_x(value):
        return lax.ppermute(value, "tensor", [(0, 1), (1, 0)])

    def over_core(value):
        return lax.ppermute(value, "dp", [(0, 1), (1, 0)])

    def over_y(value):
        return lax.ppermute(value, "expert", [(e, e ^ 1) for e in range(experts)])

    def over_z(value, shift):
        pairs = [(e, (e // 2 + shift) % ring * 2 + e % 2) for e in range(experts)]
        return lax.ppermute(value, "expert", pairs)

    def after(values, *earlier):
        return lax.optimization_barrier((values, earlier))[0]

    x = (checkpoint.astype(jnp.float32) * scales[:, None]).astype(jnp.bfloat16)
    picks = pack_picks(expert_ids, gates, width)
    m = [jnp.stack([out_grad, over_y(out_grad)])]
    u = [jnp.concatenate([x, over_x(x), picks])]
    others = [over_core(w[0]) for w in (w_gate, w_up, w_down)]
    wg, wu, wd = [jnp.concatenate([w[0], o], axis=0) for w, o in zip((w_gate, w_up, w_down), others)]
    info = jnp.stack([side, core * experts + place, (1 - core) * experts + place])
    sums, terms = [], []
    total = None
    for step in range(ring):
        last_step = step == ring - 1
        v, n = over_y(u[step]), over_x(m[step])
        way = "both" if step >= ring - 2 else "yx"[step % 2]
        if not last_step:
            u.append(over_z(u[step], 1))
            m.append(over_z(m[step], 1))
        *outs, term = run_expert(tops, way, info, u[step], v, m[step], n, wg, wu, wd)
        if not last_step:
            u[-1], m[-1] = after((u[-1], m[-1]), outs, sums[-1:])
        terms.append(term[:, 0])
        if way == "both":
            a_send, a_keep, b_send, b_keep = outs
            a_got, b_got = over_x(a_send), over_y(b_send)
            a_next, b_next = add(a_keep[1], a_got[1]), add(b_keep[1], b_got[1])
            if last_step:
                for back in range(1, ring - 1):
                    total = over_z(sums[back] if total is None else add(sums[back], total), 1)
                a_next, b_next = after((a_next, b_next), total)
                terms = after(terms, a_got, b_got)
            a = add(add(a_keep[0], a_got[0]), over_y(a_next))
            b = add(add(b_keep[0], b_got[0]), over_x(b_next))
            sums.append(jnp.concatenate([a, b], axis=0))
        else:
            first, second = (over_x, over_y) if way == "x" else (over_y, over_x)
            send, keep = outs
            got = first(send)
            sums.append(add(add(keep[0], got[0]), second(add(keep[1], got[1]))))
    total = sums[-1] if total is None else add(sums[-1], total)
    if ring > 1:
        total = add(sums[0], over_z(total, 1))
    term = jnp.stack(terms).reshape(ring, 2, 2, token_rows)
    term = term + over_x(term)
    term = jnp.stack([term[:, :, 0], over_y(term[:, :, 1])], axis=1)
    gate_out = jnp.zeros(gates.shape, jnp.float32)
    for step in range(ring):
        here = term[step] if step == 0 else over_z(term[step], -step)
        for way in range(2):
            for which in range(2):
                owner = (core ^ which) * experts + (slow + step) % ring * 2 + (fast ^ way)
                gate_out = gate_out + jnp.where(expert_ids == owner, here[way, which][:, None], 0.0)
    return (total, gate_out)


def body(checkpoint, scales, out_grad, expert_ids, gates, w_gate, w_up, w_down):
    experts = lax.axis_size("expert")
    token_rows, width = checkpoint.shape
    pairs = lax.axis_size("dp") == 2 and lax.axis_size("tensor") == 2 and experts % 2 == 0
    fits = token_rows % 128 == 0 and width % token_rows == 0
    dense = pairs and fits and expert_ids.shape[1] >= experts
    chosen = body_dense if dense else body_routed
    return chosen(checkpoint, scales, out_grad, expert_ids, gates, w_gate, w_up, w_down)


def solution(mesh):
    return jax.shard_map(
        body,
        mesh=mesh,
        in_specs=(
            P(("dp", "expert"), "tensor"),
            P(("dp", "expert")),
            P(("dp", "expert"), "tensor"),
            P(("dp", "expert"), None),
            P(("dp", "expert"), None),
            P(("dp", "expert"), "tensor", None),
            P(("dp", "expert"), "tensor", None),
            P(("dp", "expert"), "tensor", None),
        ),
        out_specs=(P(("dp", "expert"), "tensor"), P(("dp", "expert"), None)),
        check_vma=False,
    )
```

```python
import functools
import jax
import jax.numpy as jnp
from jax import lax
from jax.experimental import pallas as pl
from jax.experimental.pallas import tpu as pltpu
from jax.sharding import PartitionSpec as P


def slot_table(expert_ids, expert_count, slot_cap):
    token_rows = expert_ids.shape[0]
    pick_count = expert_ids.shape[1]
    chosen = expert_ids.reshape(-1)
    onehot = (chosen[:, None] == jnp.arange(expert_count, dtype=jnp.int32)[None, :]).astype(
        jnp.int32
    )
    earlier = jnp.cumsum(onehot, axis=0) - onehot
    position = jnp.sum(earlier * onehot, axis=1)
    slot_of = chosen * slot_cap + position
    token_ids = jnp.arange(token_rows * pick_count, dtype=jnp.int32) // pick_count
    owner = jnp.full((expert_count * slot_cap,), token_rows, jnp.int32).at[slot_of].set(token_ids)
    return (slot_of, owner)


def finish(gate_pre, up_pre, back, weight_gate, weight_up):
    sigma = jax.nn.sigmoid(gate_pre)
    swish = gate_pre * sigma
    hidden = (swish * up_pre).astype(jnp.bfloat16)
    gate_part = jnp.sum(hidden.astype(jnp.float32) * back, axis=1).astype(jnp.bfloat16)
    d_gate = (back * up_pre * sigma * (1.0 + gate_pre * (1.0 - sigma))).astype(jnp.bfloat16)
    d_up = (back * swish).astype(jnp.bfloat16)
    input_part = jnp.dot(d_gate, weight_gate, preferred_element_type=jnp.float32)
    input_part = input_part + jnp.dot(d_up, weight_up, preferred_element_type=jnp.float32)
    return (input_part.astype(jnp.bfloat16), gate_part)


def close_expert(input_part, gate_part, sources, items, model_width):
    shaped = input_part.reshape(sources, items, model_width)
    gate_shaped = gate_part.reshape(sources, items)
    summed = lax.psum_scatter(
        shaped.astype(jnp.float32).astype(jnp.bfloat16), "tensor", scatter_dimension=2, tiled=True
    )
    return (summed, gate_shaped)


def body_routed(checkpoint, scales, out_grad, expert_ids, gates, w_gate, w_up, w_down):
    expert_count = lax.axis_size("dp") * lax.axis_size("expert")
    token_rows = checkpoint.shape[0]
    pick_count = expert_ids.shape[1]
    slot_cap = min(token_rows, token_rows * pick_count // expert_count)
    weight_gate = w_gate[0]
    weight_up = w_up[0]
    weight_down = w_down[0]
    model_width = weight_gate.shape[1]
    contract = (((1,), (1,)), ((), ()))
    dequant = (checkpoint.astype(jnp.float32) * scales[:, None]).astype(jnp.bfloat16)
    slot_of, owner = slot_table(expert_ids, expert_count, slot_cap)
    full_x, full_grad = (
        lax.all_gather(dequant, "tensor", axis=1, tiled=True),
        lax.all_gather(out_grad, "tensor", axis=1, tiled=True),
    )
    send_x = jnp.take(full_x, owner, axis=0, mode="fill", fill_value=0).reshape(
        expert_count, slot_cap, model_width
    )
    send_grad = jnp.take(full_grad, owner, axis=0, mode="fill", fill_value=0).reshape(
        expert_count, slot_cap, model_width
    )
    rows_in = lax.all_to_all(send_x, ("dp", "expert"), split_axis=0, concat_axis=0, tiled=True)
    grads_in = lax.all_to_all(send_grad, ("dp", "expert"), split_axis=0, concat_axis=0, tiled=True)
    sources, items, width = rows_in.shape
    rows_flat = rows_in.reshape(sources * items, width)
    grads_flat = grads_in.reshape(sources * items, width)
    gate_pre = lax.dot_general(rows_flat, weight_gate, contract, preferred_element_type=jnp.float32)
    up_pre = lax.dot_general(rows_flat, weight_up, contract, preferred_element_type=jnp.float32)
    back = lax.dot_general(grads_flat, weight_down, contract, preferred_element_type=jnp.float32)
    input_part, gate_part = finish(gate_pre, up_pre, back, weight_gate, weight_up)
    input_part, gate_part = close_expert(input_part, gate_part, sources, items, model_width)
    back_input, back_gate = (
        lax.all_to_all(input_part, ("dp", "expert"), split_axis=0, concat_axis=0, tiled=True),
        lax.all_to_all(gate_part, ("dp", "expert"), split_axis=0, concat_axis=0, tiled=True),
    )
    share_width = back_input.shape[2]
    picked = jnp.take(back_input.reshape(expert_count * slot_cap, share_width), slot_of, axis=0)
    picked = picked.astype(jnp.float32).reshape(token_rows, pick_count, share_width)
    weighted = jnp.sum(picked * gates[:, :, None], axis=1)
    gate_pairs = (
        jnp.take(back_gate.reshape(-1), slot_of, axis=0)
        .astype(jnp.float32)
        .reshape(token_rows, pick_count)
    )
    gate_out = lax.psum(gate_pairs.astype(jnp.bfloat16), "tensor").astype(jnp.float32)
    return (weighted.astype(jnp.bfloat16), gate_out)


def expert_kernel(tops, info_ref, xs_ref, gs_ref, v_ref, n_ref, wg_ref, wu_ref, wd_ref, *outs):
    a_send, a_keep, b_send, b_keep, term_ref = outs
    f32 = jnp.float32
    contract = (((1,), (1,)), ((), ()))
    _, half, width = a_send.shape
    token_rows = 2 * half
    rows = 2 * token_rows
    units = wg_ref.shape[0] // 2
    mine = pl.ds(pl.multiple_of(info_ref[0] * width, width), width)
    other = pl.ds(pl.multiple_of((1 - info_ref[0]) * width, width), width)

    def project(first, second, w_ref):
        low = lax.dot_general(first, w_ref[:, mine], contract, preferred_element_type=f32)
        return low + lax.dot_general(second, w_ref[:, other], contract, preferred_element_type=f32)

    def weight_of(pick_rows, expert):

        def segment(kind, k):
            at = (kind * tops + k) * token_rows
            row, col = at // width, at % width
            return pick_rows[row : row + 1, col : col + token_rows].astype(f32)

        total = jnp.zeros((1, token_rows), f32)
        for k in range(tops):
            chosen = segment(0, k) == expert.astype(f32)
            total = total + jnp.where(chosen, segment(1, k) + segment(2, k), 0.0)
        return jnp.broadcast_to(total, (128, token_rows)).T[:, :1]

    x_mine = jnp.concatenate([xs_ref[token_rows:rows], v_ref[token_rows:rows]], axis=0)
    x_other = jnp.concatenate([xs_ref[:token_rows], v_ref[:token_rows]], axis=0)
    picks = xs_ref[rows:], v_ref[rows:]
    gate_pre = project(x_mine, x_other, wg_ref)
    up_pre = project(x_mine, x_other, wu_ref)
    back = project(gs_ref[...], n_ref[...], wd_ref)
    sigma = jax.nn.sigmoid(gate_pre)
    swish = gate_pre * sigma
    hidden = (swish * up_pre).astype(jnp.bfloat16)
    product = hidden.astype(f32) * back
    weights = []
    for which in range(2):
        expert = info_ref[1 + which]
        weights.append(jnp.concatenate([weight_of(part, expert) for part in picks], axis=0))
        term = jnp.sum(product[:, which * units : (which + 1) * units], axis=1, keepdims=True)
        term = term.astype(jnp.bfloat16).astype(f32)
        term_ref[which] = jnp.broadcast_to(term, (rows, 128)).T[:8]
    lane = lax.broadcasted_iota(jnp.int32, back.shape, 1)
    scaled = back * jnp.where(lane < units, weights[0], weights[1])
    d_gate = (scaled * up_pre * sigma * (1.0 + gate_pre * (1.0 - sigma))).astype(jnp.bfloat16)
    d_up = (scaled * swish).astype(jnp.bfloat16)

    def spread(cols):
        piece = jnp.dot(d_gate, wg_ref[:, cols], preferred_element_type=f32)
        piece = piece + jnp.dot(d_up, wu_ref[:, cols], preferred_element_type=f32)
        return piece.astype(jnp.bfloat16)

    far, near = spread(other), spread(mine)
    a_send[0], a_send[1] = far[:half], far[token_rows : token_rows + half]
    b_keep[1], b_send[1] = far[half:token_rows], far[token_rows + half :]
    a_keep[0], a_keep[1] = near[:half], near[token_rows : token_rows + half]
    b_keep[0], b_send[0] = near[half:token_rows], near[token_rows + half :]


def run_expert(tops, token_rows, info, xs, gs, v, n, wg, wu, wd):
    hidden, model_width = wg.shape
    rows = 2 * token_rows
    vmem = pl.BlockSpec(memory_space=pltpu.VMEM)
    share = jax.ShapeDtypeStruct((2, token_rows // 2, xs.shape[1]), jnp.bfloat16)
    return pl.pallas_call(
        functools.partial(expert_kernel, tops),
        in_specs=[pl.BlockSpec(memory_space=pltpu.SMEM)] + [vmem] * 7,
        out_specs=[vmem] * 5,
        out_shape=[share] * 4 + [jax.ShapeDtypeStruct((2, 8, rows), jnp.float32)],
        compiler_params=pltpu.CompilerParams(vmem_limit_bytes=16 * 1024 * 1024),
        cost_estimate=pl.CostEstimate(
            flops=10 * rows * hidden * model_width,
            bytes_accessed=6 * rows * model_width + 6 * hidden * model_width,
            transcendentals=rows * hidden,
        ),
    )(info, xs, gs, v, n, wg, wu, wd)


def prepare_kernel(*refs):
    sources, (own, x), held, arrived = refs[:5], refs[5:7], refs[7:12], refs[12]
    copies = [pltpu.make_async_copy(*pair, arrived.at[at]) for at, pair in enumerate(zip(sources, held))]
    for copy in copies:
        copy.start()
    for copy in copies:
        copy.wait()
    checkpoint, scales, ids, gates, out_grad = held
    f32 = jnp.float32
    token_rows, width = x.shape
    scale = jnp.broadcast_to(scales[...], (128, token_rows)).T[:, :1]
    value = (checkpoint[...].astype(f32) * scale).astype(jnp.bfloat16)
    x[...] = value
    own[:token_rows] = value
    high = gates[...].astype(jnp.bfloat16).astype(f32)
    parts = [ids[...].astype(f32), high, gates[...] - high]
    flat = [part[k : k + 1] for part in parts for k in range(part.shape[0])]
    count = own.shape[0] - 2 * token_rows
    flat += [jnp.zeros((1, token_rows), f32)] * (count * width // token_rows - len(flat))
    per = width // token_rows
    rows = [jnp.concatenate(flat[row * per : (row + 1) * per], axis=1) for row in range(count)]
    own[token_rows : token_rows + count] = jnp.concatenate(rows, axis=0).astype(jnp.bfloat16)
    own[token_rows + count :] = out_grad[...]


def stack_kernel(first, second, both):
    rows = first.shape[0]
    both[:rows] = first[...]
    both[rows:] = second[...]


def merge_kernel(own, both, xs, gs):
    token_rows = both.shape[0] // 2
    split = own.shape[0] - token_rows
    xs[:token_rows] = both[:token_rows]
    xs[token_rows:] = own[:split]
    gs[:token_rows] = own[split:]
    gs[token_rows:] = both[token_rows:]


def pick_kernel(owners, ids, *refs):
    terms, out = refs[:-1], refs[-1]
    total = jnp.zeros(out.shape, jnp.float32)
    for way, ref in enumerate(terms):
        steps, which_count, _ = ref.shape
        for step in range(steps):
            for which in range(which_count):
                owner = owners[(step * len(terms) + way) * which_count + which]
                total = total + jnp.where(ids[...] == owner, ref[step, which : which + 1], 0.0)
    out[...] = total


def join_kernel(own, both, um, xs, gs):
    token_rows = both.shape[0] // 2
    split = own.shape[0] - token_rows
    count = xs.shape[0]
    um[:token_rows] = xs[:token_rows] = both[:token_rows]
    um[token_rows:count] = xs[token_rows:] = own[:split]
    um[count : count + token_rows] = gs[:token_rows] = own[split:]
    um[count + token_rows :] = gs[token_rows:] = both[token_rows:]


def split_kernel(um, xs, gs):
    xs[...] = um[: xs.shape[0]]
    gs[...] = um[xs.shape[0] :]


def move_rows(kernel, rows, *values):
    vmem = pl.BlockSpec(memory_space=pltpu.VMEM)
    width = values[0].shape[1]
    return pl.pallas_call(
        kernel,
        in_specs=[vmem] * len(values),
        out_specs=[vmem] * len(rows),
        out_shape=[jax.ShapeDtypeStruct((count, width), jnp.bfloat16) for count in rows],
        compiler_params=pltpu.CompilerParams(vmem_limit_bytes=4 * 1024 * 1024),
        cost_estimate=pl.CostEstimate(flops=0, bytes_accessed=4 * sum(rows) * width, transcendentals=0),
    )(*values)


def add(*values):
    return sum(value.astype(jnp.float32) for value in values).astype(jnp.bfloat16)


def body_dense(checkpoint, scales, out_grad, expert_ids, gates, w_gate, w_up, w_down):
    experts = lax.axis_size("expert")
    ring = experts // 2
    core = lax.axis_index("dp")
    place = lax.axis_index("expert")
    side = lax.axis_index("tensor")
    token_rows, width = checkpoint.shape
    tops = expert_ids.shape[1]

    def over_x(value):
        return lax.ppermute(value, "tensor", [(0, 1), (1, 0)])

    def over_core(value):
        return lax.ppermute(value, "dp", [(0, 1), (1, 0)])

    def over_y(value):
        return lax.ppermute(value, "expert", [(e, e ^ 1) for e in range(experts)])

    order = [*range(0, ring, 2)][:1] + [*range(1, ring, 2)] + [*range(2, ring, 2)][::-1]
    spot = {slow: at for at, slow in enumerate(order)}

    def moved(e, shift):
        return order[(spot[e // 2] + shift) % ring] * 2 + e % 2

    def over_z(value, shift):
        return lax.ppermute(value, "expert", [(e, moved(e, shift)) for e in range(experts)])

    def after(values, *earlier):
        return lax.optimization_barrier((values, earlier))[0]

    pick_rows = -(-3 * tops * token_rows // (16 * width)) * 16
    x_count, g_count = 2 * token_rows + pick_rows, 2 * token_rows

    info = jnp.stack([side, core * experts + place, (1 - core) * experts + place])
    places = [[moved(e, step) ^ way for step in range(ring) for way in range(2)] for e in range(experts)]
    places = lax.dynamic_index_in_dim(jnp.array(places, jnp.int32), place, keepdims=False)
    owners = (places[:, None] + jnp.stack([core, 1 - core])[None, :] * experts).reshape(-1)
    checkpoint, out_grad, w_gate, w_up, w_down = after((checkpoint, out_grad, w_gate, w_up, w_down), info, owners)

    others = [over_core(w[0]) for w in (w_gate, w_up, w_down)]
    g_other = over_y(after(out_grad, others[0]))
    operands = checkpoint, scales[None, :], expert_ids.T, gates.T, out_grad
    own, x = pl.pallas_call(
        prepare_kernel,
        in_specs=[pl.BlockSpec(memory_space=pltpu.HBM)] * len(operands),
        out_specs=[pl.BlockSpec(memory_space=pltpu.VMEM)] * 2,
        out_shape=[jax.ShapeDtypeStruct((rows, width), jnp.bfloat16) for rows in (x_count, token_rows)],
        scratch_shapes=[
            *[pltpu.VMEM(value.shape, value.dtype) for value in operands],
            pltpu.SemaphoreType.DMA((len(operands),)),
        ],
        compiler_params=pltpu.CompilerParams(vmem_limit_bytes=4 * 1024 * 1024),
    )(*operands)
    near, x_other = over_z(own, 1), over_x(x)
    (both,) = move_rows(stack_kernel, (g_count,), x_other, g_other)
    both_near = over_z(both, 1)
    near = after(near, both)
    terms, shares, tokens, hops, outs = [[None] * ring for _ in range(5)]

    def hop(step):
        xs, gs = shares[step]
        tokens[step] = over_y(xs), over_x(gs)

    shares[0] = move_rows(merge_kernel, (x_count, g_count), own, both)
    hop(0)
    others = after(others, near)
    wg, wu, wd = [jnp.concatenate([w[0], far], axis=0) for w, far in zip((w_gate, w_up, w_down), others)]
    near, both_near, wg, wu, wd = lax.optimization_barrier((near, both_near, wg, wu, wd))
    um, *shares[1] = move_rows(join_kernel, (x_count + g_count, x_count, g_count), near, both_near)

    def expert(step):
        *outs, term = run_expert(tops, token_rows, info, *shares[step], *tokens[step], wg, wu, wd)
        terms[step] = term[:, 0]
        return outs

    def kernel_and_hop(step):
        outs[step] = expert(step)
        hops[step] = over_x(outs[step][0]), over_y(outs[step][2])

    moving = None
    for step in range(1, ring):
        if step > 1:
            shares[step] = move_rows(split_kernel, (x_count, g_count), um)
        hop(step)
        if step < ring - 1:
            following = over_z(um, 1)
        if step == 1:
            tokens[0] = after(tokens[0], um, shares[1])
            kernel_and_hop(0)
        if step > 1:
            hops[step - 1] = after(hops[step - 1], tokens[step])
        if step == ring - 1:
            for back in range(1, ring - 1):
                more_a, more_b = ((), ()) if moving is None else ((moving[:2],), (moving[2:],))
                (_, a_keep, _, b_keep), (a_got, b_got) = outs[back], hops[back]
                late = jnp.concatenate([add(a_keep, a_got, *more_a), add(b_keep, b_got, *more_b)])
                late = lax.optimization_barrier(after(late, shares[step]))
                moving = over_z(late, 1)
            tokens[step] = after(tokens[step], late)
        kernel_and_hop(step)
        if step < ring - 1:
            um = after(following, outs[step - 1], hops[step - 1])
    (_, a_keep, _, b_keep), (a_got, b_got) = outs[-1], hops[-1]
    term = jnp.stack(terms).reshape(ring, 2, 2, token_rows)
    term_far = over_x(term)
    a_got, b_got = after((a_got, b_got), term_far)
    a_next, b_next = add(a_keep[1], a_got[1], moving[1]), add(b_keep[1], b_got[1], moving[3])
    term = after(term + term_far, a_next, b_next)
    term = [term[step] if step == 0 else over_z(term[step], -step) for step in range(ring)]
    a = add(a_keep[0], a_got[0], moving[0], over_y(a_next))
    b = add(b_keep[0], b_got[0], moving[2], over_x(b_next))
    last = lax.optimization_barrier(jnp.concatenate([a, b]))
    moving = over_z(last, 1)
    (_, a_keep, _, b_keep), (a_got, b_got) = outs[0], after(hops[0], last)
    a0_next, b0_next = add(a_keep[1], a_got[1]), add(b_keep[1], b_got[1])
    a0, b0 = add(a_keep[0], a_got[0], over_y(a0_next)), add(b_keep[0], b_got[0], over_x(b0_next))
    term = jnp.stack(after(term, a0_next, b0_next))
    term = term[:, :, 0], over_y(term[:, :, 1])
    half = token_rows // 2
    total = jnp.concatenate([add(a0, moving[:half]), add(b0, moving[half:])])
    vmem = pl.BlockSpec(memory_space=pltpu.VMEM)
    gate_out = pl.pallas_call(
        pick_kernel,
        in_specs=[pl.BlockSpec(memory_space=pltpu.SMEM)] + [vmem] * (1 + len(term)),
        out_specs=vmem,
        out_shape=jax.ShapeDtypeStruct((tops, token_rows), jnp.float32),
        compiler_params=pltpu.CompilerParams(vmem_limit_bytes=4 * 1024 * 1024),
    )(owners, expert_ids.T, *term).T
    return (total, gate_out)


def body(checkpoint, scales, out_grad, expert_ids, gates, w_gate, w_up, w_down):
    experts = lax.axis_size("expert")
    token_rows, width = checkpoint.shape
    pairs = lax.axis_size("dp") == 2 and lax.axis_size("tensor") == 2 and experts % 2 == 0
    fits = token_rows % 128 == 0 and width % token_rows == 0
    dense = pairs and fits and expert_ids.shape[1] >= experts > 4
    chosen = body_dense if dense else body_routed
    return chosen(checkpoint, scales, out_grad, expert_ids, gates, w_gate, w_up, w_down)


def solution(mesh):
    return jax.shard_map(
        body,
        mesh=mesh,
        in_specs=(
            P(("dp", "expert"), "tensor"),
            P(("dp", "expert")),
            P(("dp", "expert"), "tensor"),
            P(("dp", "expert"), None),
            P(("dp", "expert"), None),
            P(("dp", "expert"), "tensor", None),
            P(("dp", "expert"), "tensor", None),
            P(("dp", "expert"), "tensor", None),
        ),
        out_specs=(P(("dp", "expert"), "tensor"), P(("dp", "expert"), None)),
        check_vma=False,
    )
```

```python
import functools
import jax
import jax.numpy as jnp
from jax import lax
from jax.experimental import pallas as pl
from jax.experimental.pallas import tpu as pltpu
from jax.sharding import PartitionSpec as P


def slot_table(expert_ids, expert_count, slot_cap):
    token_rows = expert_ids.shape[0]
    pick_count = expert_ids.shape[1]
    chosen = expert_ids.reshape(-1)
    onehot = (chosen[:, None] == jnp.arange(expert_count, dtype=jnp.int32)[None, :]).astype(
        jnp.int32
    )
    earlier = jnp.cumsum(onehot, axis=0) - onehot
    position = jnp.sum(earlier * onehot, axis=1)
    slot_of = chosen * slot_cap + position
    token_ids = jnp.arange(token_rows * pick_count, dtype=jnp.int32) // pick_count
    owner = jnp.full((expert_count * slot_cap,), token_rows, jnp.int32).at[slot_of].set(token_ids)
    return (slot_of, owner)


def finish(gate_pre, up_pre, back, weight_gate, weight_up):
    sigma = jax.nn.sigmoid(gate_pre)
    swish = gate_pre * sigma
    hidden = (swish * up_pre).astype(jnp.bfloat16)
    gate_part = jnp.sum(hidden.astype(jnp.float32) * back, axis=1).astype(jnp.bfloat16)
    d_gate = (back * up_pre * sigma * (1.0 + gate_pre * (1.0 - sigma))).astype(jnp.bfloat16)
    d_up = (back * swish).astype(jnp.bfloat16)
    input_part = jnp.dot(d_gate, weight_gate, preferred_element_type=jnp.float32)
    input_part = input_part + jnp.dot(d_up, weight_up, preferred_element_type=jnp.float32)
    return (input_part.astype(jnp.bfloat16), gate_part)


def close_expert(input_part, gate_part, sources, items, model_width):
    shaped = input_part.reshape(sources, items, model_width)
    gate_shaped = gate_part.reshape(sources, items)
    summed = lax.psum_scatter(
        shaped.astype(jnp.float32).astype(jnp.bfloat16), "tensor", scatter_dimension=2, tiled=True
    )
    return (summed, gate_shaped)


def body_routed(checkpoint, scales, out_grad, expert_ids, gates, w_gate, w_up, w_down):
    expert_count = lax.axis_size("dp") * lax.axis_size("expert")
    token_rows = checkpoint.shape[0]
    pick_count = expert_ids.shape[1]
    slot_cap = min(token_rows, token_rows * pick_count // expert_count)
    weight_gate = w_gate[0]
    weight_up = w_up[0]
    weight_down = w_down[0]
    model_width = weight_gate.shape[1]
    contract = (((1,), (1,)), ((), ()))
    dequant = (checkpoint.astype(jnp.float32) * scales[:, None]).astype(jnp.bfloat16)
    slot_of, owner = slot_table(expert_ids, expert_count, slot_cap)
    full_x, full_grad = (
        lax.all_gather(dequant, "tensor", axis=1, tiled=True),
        lax.all_gather(out_grad, "tensor", axis=1, tiled=True),
    )
    send_x = jnp.take(full_x, owner, axis=0, mode="fill", fill_value=0).reshape(
        expert_count, slot_cap, model_width
    )
    send_grad = jnp.take(full_grad, owner, axis=0, mode="fill", fill_value=0).reshape(
        expert_count, slot_cap, model_width
    )
    rows_in = lax.all_to_all(send_x, ("dp", "expert"), split_axis=0, concat_axis=0, tiled=True)
    grads_in = lax.all_to_all(send_grad, ("dp", "expert"), split_axis=0, concat_axis=0, tiled=True)
    sources, items, width = rows_in.shape
    rows_flat = rows_in.reshape(sources * items, width)
    grads_flat = grads_in.reshape(sources * items, width)
    gate_pre = lax.dot_general(rows_flat, weight_gate, contract, preferred_element_type=jnp.float32)
    up_pre = lax.dot_general(rows_flat, weight_up, contract, preferred_element_type=jnp.float32)
    back = lax.dot_general(grads_flat, weight_down, contract, preferred_element_type=jnp.float32)
    input_part, gate_part = finish(gate_pre, up_pre, back, weight_gate, weight_up)
    input_part, gate_part = close_expert(input_part, gate_part, sources, items, model_width)
    back_input, back_gate = (
        lax.all_to_all(input_part, ("dp", "expert"), split_axis=0, concat_axis=0, tiled=True),
        lax.all_to_all(gate_part, ("dp", "expert"), split_axis=0, concat_axis=0, tiled=True),
    )
    share_width = back_input.shape[2]
    picked = jnp.take(back_input.reshape(expert_count * slot_cap, share_width), slot_of, axis=0)
    picked = picked.astype(jnp.float32).reshape(token_rows, pick_count, share_width)
    weighted = jnp.sum(picked * gates[:, :, None], axis=1)
    gate_pairs = (
        jnp.take(back_gate.reshape(-1), slot_of, axis=0)
        .astype(jnp.float32)
        .reshape(token_rows, pick_count)
    )
    gate_out = lax.psum(gate_pairs.astype(jnp.bfloat16), "tensor").astype(jnp.float32)
    return (weighted.astype(jnp.bfloat16), gate_out)


def expert_kernel(tops, info_ref, xs_ref, gs_ref, v_ref, n_ref, wg_ref, wu_ref, wd_ref, *outs):
    a_send, a_keep, b_send, b_keep, term_ref = outs
    f32 = jnp.float32
    contract = (((1,), (1,)), ((), ()))
    _, half, width = a_send.shape
    token_rows = 2 * half
    rows = 2 * token_rows
    units = wg_ref.shape[0] // 2
    mine = pl.ds(pl.multiple_of(info_ref[0] * width, width), width)
    other = pl.ds(pl.multiple_of((1 - info_ref[0]) * width, width), width)

    def project(first, second, w_ref):
        low = lax.dot_general(first, w_ref[:, mine], contract, preferred_element_type=f32)
        return low + lax.dot_general(second, w_ref[:, other], contract, preferred_element_type=f32)

    def weight_of(pick_rows, expert):

        def segment(kind, k):
            at = (kind * tops + k) * token_rows
            row, col = at // width, at % width
            return pick_rows[row : row + 1, col : col + token_rows].astype(f32)

        total = jnp.zeros((1, token_rows), f32)
        for k in range(tops):
            chosen = segment(0, k) == expert.astype(f32)
            total = total + jnp.where(chosen, segment(1, k) + segment(2, k), 0.0)
        return jnp.broadcast_to(total, (128, token_rows)).T[:, :1]

    x_mine = jnp.concatenate([xs_ref[token_rows:rows], v_ref[token_rows:rows]], axis=0)
    x_other = jnp.concatenate([xs_ref[:token_rows], v_ref[:token_rows]], axis=0)
    picks = xs_ref[rows:], v_ref[rows:]
    gate_pre = project(x_mine, x_other, wg_ref)
    up_pre = project(x_mine, x_other, wu_ref)
    back = project(gs_ref[...], n_ref[...], wd_ref)
    sigma = jax.nn.sigmoid(gate_pre)
    swish = gate_pre * sigma
    hidden = (swish * up_pre).astype(jnp.bfloat16)
    product = hidden.astype(f32) * back
    weights = []
    for which in range(2):
        expert = info_ref[1 + which]
        weights.append(jnp.concatenate([weight_of(part, expert) for part in picks], axis=0))
        term = jnp.sum(product[:, which * units : (which + 1) * units], axis=1, keepdims=True)
        term = term.astype(jnp.bfloat16).astype(f32)
        term_ref[which] = jnp.broadcast_to(term, (rows, 128)).T[:8]
    lane = lax.broadcasted_iota(jnp.int32, back.shape, 1)
    scaled = back * jnp.where(lane < units, weights[0], weights[1])
    d_gate = (scaled * up_pre * sigma * (1.0 + gate_pre * (1.0 - sigma))).astype(jnp.bfloat16)
    d_up = (scaled * swish).astype(jnp.bfloat16)

    def spread(cols):
        piece = jnp.dot(d_gate, wg_ref[:, cols], preferred_element_type=f32)
        piece = piece + jnp.dot(d_up, wu_ref[:, cols], preferred_element_type=f32)
        return piece.astype(jnp.bfloat16)

    far, near = spread(other), spread(mine)
    a_send[0], a_send[1] = far[:half], far[token_rows : token_rows + half]
    b_keep[1], b_send[1] = far[half:token_rows], far[token_rows + half :]
    a_keep[0], a_keep[1] = near[:half], near[token_rows : token_rows + half]
    b_keep[0], b_send[0] = near[half:token_rows], near[token_rows + half :]


def run_expert(tops, token_rows, info, xs, gs, v, n, wg, wu, wd):
    hidden, model_width = wg.shape
    rows = 2 * token_rows
    vmem = pl.BlockSpec(memory_space=pltpu.VMEM)
    share = jax.ShapeDtypeStruct((2, token_rows // 2, xs.shape[1]), jnp.bfloat16)
    return pl.pallas_call(
        functools.partial(expert_kernel, tops),
        in_specs=[pl.BlockSpec(memory_space=pltpu.SMEM)] + [vmem] * 7,
        out_specs=[vmem] * 5,
        out_shape=[share] * 4 + [jax.ShapeDtypeStruct((2, 8, rows), jnp.float32)],
        compiler_params=pltpu.CompilerParams(vmem_limit_bytes=16 * 1024 * 1024),
        cost_estimate=pl.CostEstimate(
            flops=10 * rows * hidden * model_width,
            bytes_accessed=6 * rows * model_width + 6 * hidden * model_width,
            transcendentals=rows * hidden,
        ),
    )(info, xs, gs, v, n, wg, wu, wd)


def stack_kernel(x_far, g_far, ids, gates, both):
    f32 = jnp.float32
    token_rows, width = x_far.shape
    both[:token_rows] = x_far[...]
    both[token_rows : 2 * token_rows] = g_far[...]
    high = gates[...].astype(jnp.bfloat16).astype(f32)
    parts = [ids[...].astype(f32), high, gates[...] - high]
    flat = [part[k : k + 1] for part in parts for k in range(part.shape[0])]
    count = both.shape[0] - 2 * token_rows
    flat += [jnp.zeros((1, token_rows), f32)] * (count * width // token_rows - len(flat))
    per = width // token_rows
    rows = [jnp.concatenate(flat[row * per : (row + 1) * per], axis=1) for row in range(count)]
    both[2 * token_rows :] = jnp.concatenate(rows, axis=0).astype(jnp.bfloat16)


def merge_kernel(own, both, xs, gs):
    token_rows = own.shape[0] // 2
    xs[:token_rows] = both[:token_rows]
    xs[token_rows : 2 * token_rows] = own[:token_rows]
    xs[2 * token_rows :] = both[2 * token_rows :]
    gs[:token_rows] = own[token_rows:]
    gs[token_rows:] = both[token_rows : 2 * token_rows]


def join_kernel(own, both, um, xs, gs):
    merge_kernel(own, both, xs, gs)
    split = xs.shape[0]
    merge_kernel(own, both, um.at[:split], um.at[split:])


def pick_kernel(owners, ids, *refs):
    terms, out = refs[:-1], refs[-1]
    total = jnp.zeros(out.shape, jnp.float32)
    for way, ref in enumerate(terms):
        steps, which_count, _ = ref.shape
        for step in range(steps):
            for which in range(which_count):
                owner = owners[(step * len(terms) + way) * which_count + which]
                total = total + jnp.where(ids[...] == owner, ref[step, which : which + 1], 0.0)
    out[...] = total


def split_kernel(um, xs, gs):
    xs[...] = um[: xs.shape[0]]
    gs[...] = um[xs.shape[0] :]


def move_rows(kernel, rows, *values):
    vmem = pl.BlockSpec(memory_space=pltpu.VMEM)
    width = values[0].shape[1]
    return pl.pallas_call(
        kernel,
        in_specs=[vmem] * len(values),
        out_specs=[vmem] * len(rows),
        out_shape=[jax.ShapeDtypeStruct((count, width), jnp.bfloat16) for count in rows],
        compiler_params=pltpu.CompilerParams(vmem_limit_bytes=4 * 1024 * 1024),
        cost_estimate=pl.CostEstimate(flops=0, bytes_accessed=4 * sum(rows) * width, transcendentals=0),
    )(*values)


def add(*values):
    return sum(value.astype(jnp.float32) for value in values).astype(jnp.bfloat16)


def body_dense(checkpoint, scales, out_grad, expert_ids, gates, w_gate, w_up, w_down):
    experts = lax.axis_size("expert")
    ring = experts // 2
    core = lax.axis_index("dp")
    place = lax.axis_index("expert")
    side = lax.axis_index("tensor")
    token_rows, width = checkpoint.shape
    tops = expert_ids.shape[1]

    def over_x(value):
        return lax.ppermute(value, "tensor", [(0, 1), (1, 0)])

    def over_core(value):
        return lax.ppermute(value, "dp", [(0, 1), (1, 0)])

    def over_y(value):
        return lax.ppermute(value, "expert", [(e, e ^ 1) for e in range(experts)])

    order = [*range(0, ring, 2)][:1] + [*range(1, ring, 2)] + [*range(2, ring, 2)][::-1]
    spot = {slow: at for at, slow in enumerate(order)}

    def moved(e, shift):
        return order[(spot[e // 2] + shift) % ring] * 2 + e % 2

    def over_z(value, shift):
        return lax.ppermute(value, "expert", [(e, moved(e, shift)) for e in range(experts)])

    def after(values, *earlier):
        return lax.optimization_barrier((values, earlier))[0]

    pick_rows = -(-3 * tops * token_rows // (16 * width)) * 16
    x_count, g_count = 2 * token_rows + pick_rows, 2 * token_rows

    info = jnp.stack([side, core * experts + place, (1 - core) * experts + place])
    mine = sum(jnp.where(place // 2 == slow, at, 0) for at, slow in enumerate(order))
    owners = []
    for step in range(ring):
        spot_there = (mine + step) % ring
        there = sum(jnp.where(spot_there == at, slow, 0) for at, slow in enumerate(order))
        for way in range(2):
            for which in range(2):
                owners.append((core ^ which) * experts + there * 2 + (place % 2 ^ way))
    owners = jnp.stack(owners)
    checkpoint, out_grad, w_gate, w_up, w_down = after((checkpoint, out_grad, w_gate, w_up, w_down), info, owners)

    x = (checkpoint.astype(jnp.float32) * scales[:, None]).astype(jnp.bfloat16)
    own = lax.optimization_barrier(jnp.concatenate([x, out_grad]))
    near, x_other = over_z(own, 1), over_x(x)
    others = [over_core(w[0]) for w in after((w_gate, w_up, w_down), own)]
    g_other = over_y(after(out_grad, others[0]))
    ids_t, gates_t = after((expert_ids.T, gates.T), x_other)
    (both,) = move_rows(stack_kernel, (x_count,), x_other, g_other, ids_t, gates_t)
    both_near = over_z(both, 1)
    near = after(near, both)
    terms, shares, tokens, hops, outs = [[None] * ring for _ in range(5)]

    def hop(step):
        xs, gs = shares[step]
        tokens[step] = over_y(xs), over_x(gs)

    shares[0] = move_rows(merge_kernel, (x_count, g_count), own, both)
    hop(0)
    others = after(others, near)
    wg, wu, wd = [jnp.concatenate([w[0], far], axis=0) for w, far in zip((w_gate, w_up, w_down), others)]
    near, both_near, wg, wu, wd = lax.optimization_barrier((near, both_near, wg, wu, wd))
    um, *shares[1] = move_rows(join_kernel, (x_count + g_count, x_count, g_count), near, both_near)

    def expert(step):
        *outs, term = run_expert(tops, token_rows, info, *shares[step], *tokens[step], wg, wu, wd)
        terms[step] = term[:, 0]
        return outs

    def kernel_and_hop(step):
        outs[step] = expert(step)
        hops[step] = over_x(outs[step][0]), over_y(outs[step][2])

    moving = None
    for step in range(1, ring):
        if step > 1:
            shares[step] = move_rows(split_kernel, (x_count, g_count), um)
        hop(step)
        if step < ring - 1:
            following = over_z(um, 1)
        if step == 1:
            tokens[0] = after(tokens[0], um, shares[1])
            kernel_and_hop(0)
        if step > 1:
            hops[step - 1] = after(hops[step - 1], tokens[step])
        if step == ring - 1:
            for back in range(1, ring - 1):
                more_a, more_b = ((), ()) if moving is None else ((moving[:2],), (moving[2:],))
                (_, a_keep, _, b_keep), (a_got, b_got) = outs[back], hops[back]
                late = jnp.concatenate([add(a_keep, a_got, *more_a), add(b_keep, b_got, *more_b)])
                late = lax.optimization_barrier(after(late, shares[step]))
                moving = over_z(late, 1)
            tokens[step] = after(tokens[step], late)
        kernel_and_hop(step)
        if step < ring - 1:
            um = after(following, outs[step - 1], hops[step - 1])
    (_, a_keep, _, b_keep), (a_got, b_got) = outs[-1], hops[-1]
    term = jnp.stack(terms).reshape(ring, 2, 2, token_rows)
    term_far = over_x(term)
    a_got, b_got = after((a_got, b_got), term_far)
    a_next, b_next = add(a_keep[1], a_got[1], moving[1]), add(b_keep[1], b_got[1], moving[3])
    term = after(term + term_far, a_next, b_next)
    term = [term[step] if step == 0 else over_z(term[step], -step) for step in range(ring)]
    a = add(a_keep[0], a_got[0], moving[0], over_y(a_next))
    b = add(b_keep[0], b_got[0], moving[2], over_x(b_next))
    last = lax.optimization_barrier(jnp.concatenate([a, b]))
    moving = over_z(last, 1)
    (_, a_keep, _, b_keep), (a_got, b_got) = outs[0], after(hops[0], last)
    a0_next, b0_next = add(a_keep[1], a_got[1]), add(b_keep[1], b_got[1])
    a0, b0 = add(a_keep[0], a_got[0], over_y(a0_next)), add(b_keep[0], b_got[0], over_x(b0_next))
    term = jnp.stack(after(term, a0_next, b0_next))
    term = term[:, :, 0], over_y(term[:, :, 1])
    half = token_rows // 2
    total = jnp.concatenate([add(a0, moving[:half]), add(b0, moving[half:])])
    vmem = pl.BlockSpec(memory_space=pltpu.VMEM)
    gate_out = pl.pallas_call(
        pick_kernel,
        in_specs=[pl.BlockSpec(memory_space=pltpu.SMEM)] + [vmem] * (1 + len(term)),
        out_specs=vmem,
        out_shape=jax.ShapeDtypeStruct((tops, token_rows), jnp.float32),
        compiler_params=pltpu.CompilerParams(vmem_limit_bytes=4 * 1024 * 1024),
    )(owners, expert_ids.T, *term).T
    return (total, gate_out)


def body(checkpoint, scales, out_grad, expert_ids, gates, w_gate, w_up, w_down):
    experts = lax.axis_size("expert")
    token_rows, width = checkpoint.shape
    pairs = lax.axis_size("dp") == 2 and lax.axis_size("tensor") == 2 and experts % 2 == 0
    fits = token_rows % 128 == 0 and width % token_rows == 0
    dense = pairs and fits and expert_ids.shape[1] >= experts > 4
    chosen = body_dense if dense else body_routed
    return chosen(checkpoint, scales, out_grad, expert_ids, gates, w_gate, w_up, w_down)


def solution(mesh):
    return jax.shard_map(
        body,
        mesh=mesh,
        in_specs=(
            P(("dp", "expert"), "tensor"),
            P(("dp", "expert")),
            P(("dp", "expert"), "tensor"),
            P(("dp", "expert"), None),
            P(("dp", "expert"), None),
            P(("dp", "expert"), "tensor", None),
            P(("dp", "expert"), "tensor", None),
            P(("dp", "expert"), "tensor", None),
        ),
        out_specs=(P(("dp", "expert"), "tensor"), P(("dp", "expert"), None)),
        check_vma=False,
    )
```

```python
import functools
import jax
import jax.numpy as jnp
from jax import lax
from jax.experimental import pallas as pl
from jax.experimental.pallas import tpu as pltpu
from jax.sharding import PartitionSpec as P


def slot_table(expert_ids, expert_count, slot_cap):
    token_rows = expert_ids.shape[0]
    pick_count = expert_ids.shape[1]
    chosen = expert_ids.reshape(-1)
    onehot = (chosen[:, None] == jnp.arange(expert_count, dtype=jnp.int32)[None, :]).astype(
        jnp.int32
    )
    earlier = jnp.cumsum(onehot, axis=0) - onehot
    position = jnp.sum(earlier * onehot, axis=1)
    slot_of = chosen * slot_cap + position
    token_ids = jnp.arange(token_rows * pick_count, dtype=jnp.int32) // pick_count
    owner = jnp.full((expert_count * slot_cap,), token_rows, jnp.int32).at[slot_of].set(token_ids)
    return (slot_of, owner)


def finish(gate_pre, up_pre, back, weight_gate, weight_up):
    sigma = jax.nn.sigmoid(gate_pre)
    swish = gate_pre * sigma
    hidden = (swish * up_pre).astype(jnp.bfloat16)
    gate_part = jnp.sum(hidden.astype(jnp.float32) * back, axis=1).astype(jnp.bfloat16)
    d_gate = (back * up_pre * sigma * (1.0 + gate_pre * (1.0 - sigma))).astype(jnp.bfloat16)
    d_up = (back * swish).astype(jnp.bfloat16)
    input_part = jnp.dot(d_gate, weight_gate, preferred_element_type=jnp.float32)
    input_part = input_part + jnp.dot(d_up, weight_up, preferred_element_type=jnp.float32)
    return (input_part.astype(jnp.bfloat16), gate_part)


def close_expert(input_part, gate_part, sources, items, model_width):
    shaped = input_part.reshape(sources, items, model_width)
    gate_shaped = gate_part.reshape(sources, items)
    summed = lax.psum_scatter(
        shaped.astype(jnp.float32).astype(jnp.bfloat16), "tensor", scatter_dimension=2, tiled=True
    )
    return (summed, gate_shaped)


def body_routed(checkpoint, scales, out_grad, expert_ids, gates, w_gate, w_up, w_down):
    expert_count = lax.axis_size("dp") * lax.axis_size("expert")
    token_rows = checkpoint.shape[0]
    pick_count = expert_ids.shape[1]
    slot_cap = min(token_rows, token_rows * pick_count // expert_count)
    weight_gate = w_gate[0]
    weight_up = w_up[0]
    weight_down = w_down[0]
    model_width = weight_gate.shape[1]
    contract = (((1,), (1,)), ((), ()))
    dequant = (checkpoint.astype(jnp.float32) * scales[:, None]).astype(jnp.bfloat16)
    slot_of, owner = slot_table(expert_ids, expert_count, slot_cap)
    full_x, full_grad = (
        lax.all_gather(dequant, "tensor", axis=1, tiled=True),
        lax.all_gather(out_grad, "tensor", axis=1, tiled=True),
    )
    send_x = jnp.take(full_x, owner, axis=0, mode="fill", fill_value=0).reshape(
        expert_count, slot_cap, model_width
    )
    send_grad = jnp.take(full_grad, owner, axis=0, mode="fill", fill_value=0).reshape(
        expert_count, slot_cap, model_width
    )
    rows_in = lax.all_to_all(send_x, ("dp", "expert"), split_axis=0, concat_axis=0, tiled=True)
    grads_in = lax.all_to_all(send_grad, ("dp", "expert"), split_axis=0, concat_axis=0, tiled=True)
    sources, items, width = rows_in.shape
    rows_flat = rows_in.reshape(sources * items, width)
    grads_flat = grads_in.reshape(sources * items, width)
    gate_pre = lax.dot_general(rows_flat, weight_gate, contract, preferred_element_type=jnp.float32)
    up_pre = lax.dot_general(rows_flat, weight_up, contract, preferred_element_type=jnp.float32)
    back = lax.dot_general(grads_flat, weight_down, contract, preferred_element_type=jnp.float32)
    input_part, gate_part = finish(gate_pre, up_pre, back, weight_gate, weight_up)
    input_part, gate_part = close_expert(input_part, gate_part, sources, items, model_width)
    back_input, back_gate = (
        lax.all_to_all(input_part, ("dp", "expert"), split_axis=0, concat_axis=0, tiled=True),
        lax.all_to_all(gate_part, ("dp", "expert"), split_axis=0, concat_axis=0, tiled=True),
    )
    share_width = back_input.shape[2]
    picked = jnp.take(back_input.reshape(expert_count * slot_cap, share_width), slot_of, axis=0)
    picked = picked.astype(jnp.float32).reshape(token_rows, pick_count, share_width)
    weighted = jnp.sum(picked * gates[:, :, None], axis=1)
    gate_pairs = (
        jnp.take(back_gate.reshape(-1), slot_of, axis=0)
        .astype(jnp.float32)
        .reshape(token_rows, pick_count)
    )
    gate_out = lax.psum(gate_pairs.astype(jnp.bfloat16), "tensor").astype(jnp.float32)
    return (weighted.astype(jnp.bfloat16), gate_out)


def expert_kernel(tops, info_ref, xs_ref, gs_ref, v_ref, n_ref, wg_ref, wu_ref, wd_ref, *outs):
    a_send, a_keep, b_send, b_keep, term_ref = outs
    f32 = jnp.float32
    contract = (((1,), (1,)), ((), ()))
    _, half, width = a_send.shape
    token_rows = 2 * half
    rows = 2 * token_rows
    units = wg_ref.shape[0] // 2
    mine = pl.ds(pl.multiple_of(info_ref[0] * width, width), width)
    other = pl.ds(pl.multiple_of((1 - info_ref[0]) * width, width), width)

    def project(first, second, w_ref):
        low = lax.dot_general(first, w_ref[:, mine], contract, preferred_element_type=f32)
        return low + lax.dot_general(second, w_ref[:, other], contract, preferred_element_type=f32)

    def weight_of(pick_rows, expert):

        def segment(kind, k):
            at = (kind * tops + k) * token_rows
            row, col = at // width, at % width
            return pick_rows[row : row + 1, col : col + token_rows].astype(f32)

        total = jnp.zeros((1, token_rows), f32)
        for k in range(tops):
            chosen = segment(0, k) == expert.astype(f32)
            total = total + jnp.where(chosen, segment(1, k) + segment(2, k), 0.0)
        return jnp.broadcast_to(total, (128, token_rows)).T[:, :1]

    x_mine = jnp.concatenate([xs_ref[token_rows:rows], v_ref[token_rows:rows]], axis=0)
    x_other = jnp.concatenate([xs_ref[:token_rows], v_ref[:token_rows]], axis=0)
    picks = xs_ref[rows:], v_ref[rows:]
    gate_pre = project(x_mine, x_other, wg_ref)
    up_pre = project(x_mine, x_other, wu_ref)
    back = project(gs_ref[...], n_ref[...], wd_ref)
    sigma = jax.nn.sigmoid(gate_pre)
    swish = gate_pre * sigma
    hidden = (swish * up_pre).astype(jnp.bfloat16)
    product = hidden.astype(f32) * back
    weights = []
    for which in range(2):
        expert = info_ref[1 + which]
        weights.append(jnp.concatenate([weight_of(part, expert) for part in picks], axis=0))
        term = jnp.sum(product[:, which * units : (which + 1) * units], axis=1, keepdims=True)
        term = term.astype(jnp.bfloat16).astype(f32)
        term_ref[which] = jnp.broadcast_to(term, (rows, 128)).T[:8]
    lane = lax.broadcasted_iota(jnp.int32, back.shape, 1)
    scaled = back * jnp.where(lane < units, weights[0], weights[1])
    d_gate = (scaled * up_pre * sigma * (1.0 + gate_pre * (1.0 - sigma))).astype(jnp.bfloat16)
    d_up = (scaled * swish).astype(jnp.bfloat16)

    def spread(cols):
        piece = jnp.dot(d_gate, wg_ref[:, cols], preferred_element_type=f32)
        piece = piece + jnp.dot(d_up, wu_ref[:, cols], preferred_element_type=f32)
        return piece.astype(jnp.bfloat16)

    far, near = spread(other), spread(mine)
    a_send[0], a_send[1] = far[:half], far[token_rows : token_rows + half]
    b_keep[1], b_send[1] = far[half:token_rows], far[token_rows + half :]
    a_keep[0], a_keep[1] = near[:half], near[token_rows : token_rows + half]
    b_keep[0], b_send[0] = near[half:token_rows], near[token_rows + half :]


def run_expert(tops, token_rows, info, xs, gs, v, n, wg, wu, wd):
    hidden, model_width = wg.shape
    rows = 2 * token_rows
    vmem = pl.BlockSpec(memory_space=pltpu.VMEM)
    share = jax.ShapeDtypeStruct((2, token_rows // 2, xs.shape[1]), jnp.bfloat16)
    return pl.pallas_call(
        functools.partial(expert_kernel, tops),
        in_specs=[pl.BlockSpec(memory_space=pltpu.SMEM)] + [vmem] * 7,
        out_specs=[vmem] * 5,
        out_shape=[share] * 4 + [jax.ShapeDtypeStruct((2, 8, rows), jnp.float32)],
        compiler_params=pltpu.CompilerParams(vmem_limit_bytes=16 * 1024 * 1024),
        cost_estimate=pl.CostEstimate(
            flops=10 * rows * hidden * model_width,
            bytes_accessed=6 * rows * model_width + 6 * hidden * model_width,
            transcendentals=rows * hidden,
        ),
    )(info, xs, gs, v, n, wg, wu, wd)


def picks_kernel(ids, gates, picks):
    f32 = jnp.float32
    count, width = picks.shape
    token_rows = ids.shape[1]
    high = gates[...].astype(jnp.bfloat16).astype(f32)
    parts = [ids[...].astype(f32), high, gates[...] - high]
    flat = [part[k : k + 1] for part in parts for k in range(part.shape[0])]
    flat += [jnp.zeros((1, token_rows), f32)] * (count * width // token_rows - len(flat))
    per = width // token_rows
    rows = [jnp.concatenate(flat[row * per : (row + 1) * per], axis=1) for row in range(count)]
    picks[...] = jnp.concatenate(rows, axis=0).astype(jnp.bfloat16)


def stack_kernel(x_far, g_far, picks, both):
    token_rows = x_far.shape[0]
    both[:token_rows] = x_far[...]
    both[token_rows : 2 * token_rows] = g_far[...]
    both[2 * token_rows :] = picks[...]


def merge_kernel(own, both, xs, gs):
    token_rows = own.shape[0] // 2
    xs[:token_rows] = both[:token_rows]
    xs[token_rows : 2 * token_rows] = own[:token_rows]
    xs[2 * token_rows :] = both[2 * token_rows :]
    gs[:token_rows] = own[token_rows:]
    gs[token_rows:] = both[token_rows : 2 * token_rows]


def join_kernel(own, both, um, xs, gs):
    merge_kernel(own, both, xs, gs)
    split = xs.shape[0]
    merge_kernel(own, both, um.at[:split], um.at[split:])


def pick_kernel(owners, ids, *refs):
    terms, out = refs[:-1], refs[-1]
    total = jnp.zeros(out.shape, jnp.float32)
    for way, ref in enumerate(terms):
        steps, which_count, _ = ref.shape
        for step in range(steps):
            for which in range(which_count):
                owner = owners[(step * len(terms) + way) * which_count + which]
                total = total + jnp.where(ids[...] == owner, ref[step, which : which + 1], 0.0)
    out[...] = total


def split_kernel(um, xs, gs):
    xs[...] = um[: xs.shape[0]]
    gs[...] = um[xs.shape[0] :]


def move_rows(kernel, rows, width, *values):
    vmem = pl.BlockSpec(memory_space=pltpu.VMEM)
    return pl.pallas_call(
        kernel,
        in_specs=[vmem] * len(values),
        out_specs=[vmem] * len(rows),
        out_shape=[jax.ShapeDtypeStruct((count, width), jnp.bfloat16) for count in rows],
        compiler_params=pltpu.CompilerParams(vmem_limit_bytes=4 * 1024 * 1024),
        cost_estimate=pl.CostEstimate(flops=0, bytes_accessed=4 * sum(rows) * width, transcendentals=0),
    )(*values)


def add(*values):
    return sum(value.astype(jnp.float32) for value in values).astype(jnp.bfloat16)


def body_dense(checkpoint, scales, out_grad, expert_ids, gates, w_gate, w_up, w_down):
    experts = lax.axis_size("expert")
    ring = experts // 2
    core = lax.axis_index("dp")
    place = lax.axis_index("expert")
    side = lax.axis_index("tensor")
    token_rows, width = checkpoint.shape
    tops = expert_ids.shape[1]

    def over_x(value):
        return lax.ppermute(value, "tensor", [(0, 1), (1, 0)])

    def over_core(value):
        return lax.ppermute(value, "dp", [(0, 1), (1, 0)])

    def over_y(value):
        return lax.ppermute(value, "expert", [(e, e ^ 1) for e in range(experts)])

    order = [*range(0, ring, 2)][:1] + [*range(1, ring, 2)] + [*range(2, ring, 2)][::-1]
    spot = {slow: at for at, slow in enumerate(order)}

    def moved(e, shift):
        return order[(spot[e // 2] + shift) % ring] * 2 + e % 2

    def over_z(value, shift):
        return lax.ppermute(value, "expert", [(e, moved(e, shift)) for e in range(experts)])

    def after(values, *earlier):
        return lax.optimization_barrier((values, earlier))[0]

    pick_rows = -(-3 * tops * token_rows // (16 * width)) * 16
    x_count, g_count = 2 * token_rows + pick_rows, 2 * token_rows

    info = jnp.stack([side, core * experts + place, (1 - core) * experts + place])
    mine = sum(jnp.where(place // 2 == slow, at, 0) for at, slow in enumerate(order))
    owners = []
    for step in range(ring):
        spot_there = (mine + step) % ring
        there = sum(jnp.where(spot_there == at, slow, 0) for at, slow in enumerate(order))
        for way in range(2):
            for which in range(2):
                owners.append((core ^ which) * experts + there * 2 + (place % 2 ^ way))
    owners = jnp.stack(owners)
    checkpoint, out_grad, w_gate, w_up, w_down = after((checkpoint, out_grad, w_gate, w_up, w_down), info, owners)

    x = (checkpoint.astype(jnp.float32) * scales[:, None]).astype(jnp.bfloat16)
    own = lax.optimization_barrier(jnp.concatenate([x, out_grad]))
    near, x_other = over_z(own, 1), over_x(x)
    others = [over_core(w[0]) for w in after((w_gate, w_up, w_down), own)]
    g_other = over_y(after(out_grad, others[0]))
    ids_t, gates_t = after((expert_ids.T, gates.T), others[0])
    (picks,) = move_rows(picks_kernel, (pick_rows,), width, ids_t, gates_t)
    picks, x_other = lax.optimization_barrier((picks, x_other))
    (both,) = move_rows(stack_kernel, (x_count,), width, x_other, g_other, picks)
    both_near = over_z(both, 1)
    near = after(near, both)
    terms, shares, tokens, hops, outs = [[None] * ring for _ in range(5)]

    def hop(step):
        xs, gs = shares[step]
        tokens[step] = over_y(xs), over_x(gs)

    shares[0] = move_rows(merge_kernel, (x_count, g_count), width, own, both)
    hop(0)
    others = after(others, near)
    wg, wu, wd = [jnp.concatenate([w[0], far], axis=0) for w, far in zip((w_gate, w_up, w_down), others)]
    near, both_near, wg, wu, wd = lax.optimization_barrier((near, both_near, wg, wu, wd))
    um, *shares[1] = move_rows(join_kernel, (x_count + g_count, x_count, g_count), width, near, both_near)

    def expert(step):
        *outs, term = run_expert(tops, token_rows, info, *shares[step], *tokens[step], wg, wu, wd)
        terms[step] = term[:, 0]
        return outs

    def kernel_and_hop(step):
        outs[step] = expert(step)
        hops[step] = over_x(outs[step][0]), over_y(outs[step][2])

    moving = None
    for step in range(1, ring):
        if step > 1:
            shares[step] = move_rows(split_kernel, (x_count, g_count), width, um)
        hop(step)
        if step < ring - 1:
            following = over_z(um, 1)
        if step == 1:
            tokens[0] = after(tokens[0], um, shares[1])
            kernel_and_hop(0)
        if step > 1:
            hops[step - 1] = after(hops[step - 1], tokens[step])
        if step == ring - 1:
            for back in range(1, ring - 1):
                more_a, more_b = ((), ()) if moving is None else ((moving[:2],), (moving[2:],))
                (_, a_keep, _, b_keep), (a_got, b_got) = outs[back], hops[back]
                late = jnp.concatenate([add(a_keep, a_got, *more_a), add(b_keep, b_got, *more_b)])
                late = lax.optimization_barrier(after(late, shares[step]))
                moving = over_z(late, 1)
            tokens[step] = after(tokens[step], late)
        kernel_and_hop(step)
        if step < ring - 1:
            um = after(following, outs[step - 1], hops[step - 1])
    (_, a_keep, _, b_keep), (a_got, b_got) = outs[-1], hops[-1]
    term = jnp.stack(terms).reshape(ring, 2, 2, token_rows)
    term_far = over_x(term)
    a_got, b_got = after((a_got, b_got), term_far)
    a_next, b_next = add(a_keep[1], a_got[1], moving[1]), add(b_keep[1], b_got[1], moving[3])
    term = after(term + term_far, a_next, b_next)
    term = [term[step] if step == 0 else over_z(term[step], -step) for step in range(ring)]
    a = add(a_keep[0], a_got[0], moving[0], over_y(a_next))
    b = add(b_keep[0], b_got[0], moving[2], over_x(b_next))
    last = lax.optimization_barrier(jnp.concatenate([a, b]))
    moving = over_z(last, 1)
    (_, a_keep, _, b_keep), (a_got, b_got) = outs[0], after(hops[0], last)
    a0_next, b0_next = add(a_keep[1], a_got[1]), add(b_keep[1], b_got[1])
    a0, b0 = add(a_keep[0], a_got[0], over_y(a0_next)), add(b_keep[0], b_got[0], over_x(b0_next))
    term = jnp.stack(after(term, a0_next, b0_next))
    term = term[:, :, 0], over_y(term[:, :, 1])
    half = token_rows // 2
    total = jnp.concatenate([add(a0, moving[:half]), add(b0, moving[half:])])
    vmem = pl.BlockSpec(memory_space=pltpu.VMEM)
    gate_out = pl.pallas_call(
        pick_kernel,
        in_specs=[pl.BlockSpec(memory_space=pltpu.SMEM)] + [vmem] * (1 + len(term)),
        out_specs=vmem,
        out_shape=jax.ShapeDtypeStruct((tops, token_rows), jnp.float32),
        compiler_params=pltpu.CompilerParams(vmem_limit_bytes=4 * 1024 * 1024),
    )(owners, expert_ids.T, *term).T
    return (total, gate_out)


def body(checkpoint, scales, out_grad, expert_ids, gates, w_gate, w_up, w_down):
    experts = lax.axis_size("expert")
    token_rows, width = checkpoint.shape
    pairs = lax.axis_size("dp") == 2 and lax.axis_size("tensor") == 2 and experts % 2 == 0
    fits = token_rows % 128 == 0 and width % token_rows == 0
    dense = pairs and fits and expert_ids.shape[1] >= experts > 4
    chosen = body_dense if dense else body_routed
    return chosen(checkpoint, scales, out_grad, expert_ids, gates, w_gate, w_up, w_down)


def solution(mesh):
    return jax.shard_map(
        body,
        mesh=mesh,
        in_specs=(
            P(("dp", "expert"), "tensor"),
            P(("dp", "expert")),
            P(("dp", "expert"), "tensor"),
            P(("dp", "expert"), None),
            P(("dp", "expert"), None),
            P(("dp", "expert"), "tensor", None),
            P(("dp", "expert"), "tensor", None),
            P(("dp", "expert"), "tensor", None),
        ),
        out_specs=(P(("dp", "expert"), "tensor"), P(("dp", "expert"), None)),
        check_vma=False,
    )
```

```python
import functools
import jax
import jax.numpy as jnp
from jax import lax
from jax.experimental import pallas as pl
from jax.experimental.pallas import tpu as pltpu
from jax.sharding import PartitionSpec as P


def slot_table(expert_ids, expert_count, slot_cap):
    token_rows = expert_ids.shape[0]
    pick_count = expert_ids.shape[1]
    chosen = expert_ids.reshape(-1)
    onehot = (chosen[:, None] == jnp.arange(expert_count, dtype=jnp.int32)[None, :]).astype(
        jnp.int32
    )
    earlier = jnp.cumsum(onehot, axis=0) - onehot
    position = jnp.sum(earlier * onehot, axis=1)
    slot_of = chosen * slot_cap + position
    token_ids = jnp.arange(token_rows * pick_count, dtype=jnp.int32) // pick_count
    owner = jnp.full((expert_count * slot_cap,), token_rows, jnp.int32).at[slot_of].set(token_ids)
    return (slot_of, owner)


def finish(gate_pre, up_pre, back, weight_gate, weight_up):
    sigma = jax.nn.sigmoid(gate_pre)
    swish = gate_pre * sigma
    hidden = (swish * up_pre).astype(jnp.bfloat16)
    gate_part = jnp.sum(hidden.astype(jnp.float32) * back, axis=1).astype(jnp.bfloat16)
    d_gate = (back * up_pre * sigma * (1.0 + gate_pre * (1.0 - sigma))).astype(jnp.bfloat16)
    d_up = (back * swish).astype(jnp.bfloat16)
    input_part = jnp.dot(d_gate, weight_gate, preferred_element_type=jnp.float32)
    input_part = input_part + jnp.dot(d_up, weight_up, preferred_element_type=jnp.float32)
    return (input_part.astype(jnp.bfloat16), gate_part)


def close_expert(input_part, gate_part, sources, items, model_width):
    shaped = input_part.reshape(sources, items, model_width)
    gate_shaped = gate_part.reshape(sources, items)
    summed = lax.psum_scatter(
        shaped.astype(jnp.float32).astype(jnp.bfloat16), "tensor", scatter_dimension=2, tiled=True
    )
    return (summed, gate_shaped)


def body_routed(checkpoint, scales, out_grad, expert_ids, gates, w_gate, w_up, w_down):
    expert_count = lax.axis_size("dp") * lax.axis_size("expert")
    token_rows = checkpoint.shape[0]
    pick_count = expert_ids.shape[1]
    slot_cap = min(token_rows, token_rows * pick_count // expert_count)
    weight_gate = w_gate[0]
    weight_up = w_up[0]
    weight_down = w_down[0]
    model_width = weight_gate.shape[1]
    contract = (((1,), (1,)), ((), ()))
    dequant = (checkpoint.astype(jnp.float32) * scales[:, None]).astype(jnp.bfloat16)
    slot_of, owner = slot_table(expert_ids, expert_count, slot_cap)
    full_x, full_grad = (
        lax.all_gather(dequant, "tensor", axis=1, tiled=True),
        lax.all_gather(out_grad, "tensor", axis=1, tiled=True),
    )
    send_x = jnp.take(full_x, owner, axis=0, mode="fill", fill_value=0).reshape(
        expert_count, slot_cap, model_width
    )
    send_grad = jnp.take(full_grad, owner, axis=0, mode="fill", fill_value=0).reshape(
        expert_count, slot_cap, model_width
    )
    rows_in = lax.all_to_all(send_x, ("dp", "expert"), split_axis=0, concat_axis=0, tiled=True)
    grads_in = lax.all_to_all(send_grad, ("dp", "expert"), split_axis=0, concat_axis=0, tiled=True)
    sources, items, width = rows_in.shape
    rows_flat = rows_in.reshape(sources * items, width)
    grads_flat = grads_in.reshape(sources * items, width)
    gate_pre = lax.dot_general(rows_flat, weight_gate, contract, preferred_element_type=jnp.float32)
    up_pre = lax.dot_general(rows_flat, weight_up, contract, preferred_element_type=jnp.float32)
    back = lax.dot_general(grads_flat, weight_down, contract, preferred_element_type=jnp.float32)
    input_part, gate_part = finish(gate_pre, up_pre, back, weight_gate, weight_up)
    input_part, gate_part = close_expert(input_part, gate_part, sources, items, model_width)
    back_input, back_gate = (
        lax.all_to_all(input_part, ("dp", "expert"), split_axis=0, concat_axis=0, tiled=True),
        lax.all_to_all(gate_part, ("dp", "expert"), split_axis=0, concat_axis=0, tiled=True),
    )
    share_width = back_input.shape[2]
    picked = jnp.take(back_input.reshape(expert_count * slot_cap, share_width), slot_of, axis=0)
    picked = picked.astype(jnp.float32).reshape(token_rows, pick_count, share_width)
    weighted = jnp.sum(picked * gates[:, :, None], axis=1)
    gate_pairs = (
        jnp.take(back_gate.reshape(-1), slot_of, axis=0)
        .astype(jnp.float32)
        .reshape(token_rows, pick_count)
    )
    gate_out = lax.psum(gate_pairs.astype(jnp.bfloat16), "tensor").astype(jnp.float32)
    return (weighted.astype(jnp.bfloat16), gate_out)


def expert_kernel(tops, info_ref, xs_ref, gs_ref, v_ref, n_ref, wg_ref, wu_ref, wd_ref, *outs):
    a_send, a_keep, b_send, b_keep, term_ref = outs
    f32 = jnp.float32
    contract = (((1,), (1,)), ((), ()))
    _, half, width = a_send.shape
    token_rows = 2 * half
    rows = 2 * token_rows
    units = wg_ref.shape[0] // 2
    mine = pl.ds(pl.multiple_of(info_ref[0] * width, width), width)
    other = pl.ds(pl.multiple_of((1 - info_ref[0]) * width, width), width)

    def project(first, second, w_ref):
        low = lax.dot_general(first, w_ref[:, mine], contract, preferred_element_type=f32)
        return low + lax.dot_general(second, w_ref[:, other], contract, preferred_element_type=f32)

    def weight_of(pick_rows, expert):

        def segment(kind, k):
            at = (kind * tops + k) * token_rows
            row, col = at // width, at % width
            return pick_rows[row : row + 1, col : col + token_rows].astype(f32)

        total = jnp.zeros((1, token_rows), f32)
        for k in range(tops):
            chosen = segment(0, k) == expert.astype(f32)
            total = total + jnp.where(chosen, segment(1, k) + segment(2, k), 0.0)
        return jnp.broadcast_to(total, (128, token_rows)).T[:, :1]

    x_mine = jnp.concatenate([xs_ref[token_rows:rows], v_ref[token_rows:rows]], axis=0)
    x_other = jnp.concatenate([xs_ref[:token_rows], v_ref[:token_rows]], axis=0)
    picks = xs_ref[rows:], v_ref[rows:]
    gate_pre = project(x_mine, x_other, wg_ref)
    up_pre = project(x_mine, x_other, wu_ref)
    back = project(gs_ref[...], n_ref[...], wd_ref)
    sigma = jax.nn.sigmoid(gate_pre)
    swish = gate_pre * sigma
    hidden = (swish * up_pre).astype(jnp.bfloat16)
    product = hidden.astype(f32) * back
    weights = []
    for which in range(2):
        expert = info_ref[1 + which]
        weights.append(jnp.concatenate([weight_of(part, expert) for part in picks], axis=0))
        term = jnp.sum(product[:, which * units : (which + 1) * units], axis=1, keepdims=True)
        term = term.astype(jnp.bfloat16).astype(f32)
        term_ref[which] = jnp.broadcast_to(term, (rows, 128)).T[:8]
    lane = lax.broadcasted_iota(jnp.int32, back.shape, 1)
    scaled = back * jnp.where(lane < units, weights[0], weights[1])
    d_gate = (scaled * up_pre * sigma * (1.0 + gate_pre * (1.0 - sigma))).astype(jnp.bfloat16)
    d_up = (scaled * swish).astype(jnp.bfloat16)

    def spread(cols):
        piece = jnp.dot(d_gate, wg_ref[:, cols], preferred_element_type=f32)
        piece = piece + jnp.dot(d_up, wu_ref[:, cols], preferred_element_type=f32)
        return piece.astype(jnp.bfloat16)

    far, near = spread(other), spread(mine)
    a_send[0], a_send[1] = far[:half], far[token_rows : token_rows + half]
    b_keep[1], b_send[1] = far[half:token_rows], far[token_rows + half :]
    a_keep[0], a_keep[1] = near[:half], near[token_rows : token_rows + half]
    b_keep[0], b_send[0] = near[half:token_rows], near[token_rows + half :]


def run_expert(tops, token_rows, info, xs, gs, v, n, wg, wu, wd):
    hidden, model_width = wg.shape
    rows = 2 * token_rows
    vmem = pl.BlockSpec(memory_space=pltpu.VMEM)
    share = jax.ShapeDtypeStruct((2, token_rows // 2, xs.shape[1]), jnp.bfloat16)
    return pl.pallas_call(
        functools.partial(expert_kernel, tops),
        in_specs=[pl.BlockSpec(memory_space=pltpu.SMEM)] + [vmem] * 7,
        out_specs=[vmem] * 5,
        out_shape=[share] * 4 + [jax.ShapeDtypeStruct((2, 8, rows), jnp.float32)],
        compiler_params=pltpu.CompilerParams(vmem_limit_bytes=16 * 1024 * 1024),
        cost_estimate=pl.CostEstimate(
            flops=10 * rows * hidden * model_width,
            bytes_accessed=6 * rows * model_width + 6 * hidden * model_width,
            transcendentals=rows * hidden,
        ),
    )(info, xs, gs, v, n, wg, wu, wd)


def picks_kernel(ids, gates, picks):
    f32 = jnp.float32
    count, width = picks.shape
    token_rows = ids.shape[1]
    high = gates[...].astype(jnp.bfloat16).astype(f32)
    parts = [ids[...].astype(f32), high, gates[...] - high]
    flat = [part[k : k + 1] for part in parts for k in range(part.shape[0])]
    flat += [jnp.zeros((1, token_rows), f32)] * (count * width // token_rows - len(flat))
    per = width // token_rows
    rows = [jnp.concatenate(flat[row * per : (row + 1) * per], axis=1) for row in range(count)]
    picks[...] = jnp.concatenate(rows, axis=0).astype(jnp.bfloat16)


def stack_kernel(x_far, g_far, picks, both):
    token_rows = x_far.shape[0]
    both[:token_rows] = x_far[...]
    both[token_rows : 2 * token_rows] = g_far[...]
    both[2 * token_rows :] = picks[...]


def merge_kernel(x, g, both, xs, gs):
    token_rows = x.shape[0]
    xs[:token_rows] = both[:token_rows]
    xs[token_rows : 2 * token_rows] = x[...]
    xs[2 * token_rows :] = both[2 * token_rows :]
    gs[:token_rows] = g[...]
    gs[token_rows:] = both[token_rows : 2 * token_rows]


def join_kernel(x, g, both, um, xs, gs):
    merge_kernel(x, g, both, xs, gs)
    split = xs.shape[0]
    merge_kernel(x, g, both, um.at[:split], um.at[split:])


def pick_kernel(owners, ids, *refs):
    terms, out = refs[:-1], refs[-1]
    total = jnp.zeros(out.shape, jnp.float32)
    for way, ref in enumerate(terms):
        steps, which_count, _ = ref.shape
        for step in range(steps):
            for which in range(which_count):
                owner = owners[(step * len(terms) + way) * which_count + which]
                total = total + jnp.where(ids[...] == owner, ref[step, which : which + 1], 0.0)
    out[...] = total


def split_kernel(um, xs, gs):
    xs[...] = um[: xs.shape[0]]
    gs[...] = um[xs.shape[0] :]


def move_rows(kernel, rows, width, *values):
    vmem = pl.BlockSpec(memory_space=pltpu.VMEM)
    return pl.pallas_call(
        kernel,
        in_specs=[vmem] * len(values),
        out_specs=[vmem] * len(rows),
        out_shape=[jax.ShapeDtypeStruct((count, width), jnp.bfloat16) for count in rows],
        compiler_params=pltpu.CompilerParams(vmem_limit_bytes=4 * 1024 * 1024),
        cost_estimate=pl.CostEstimate(flops=0, bytes_accessed=4 * sum(rows) * width, transcendentals=0),
    )(*values)


def add(*values):
    return sum(value.astype(jnp.float32) for value in values).astype(jnp.bfloat16)


def body_dense(checkpoint, scales, out_grad, expert_ids, gates, w_gate, w_up, w_down):
    experts = lax.axis_size("expert")
    ring = experts // 2
    core = lax.axis_index("dp")
    place = lax.axis_index("expert")
    side = lax.axis_index("tensor")
    token_rows, width = checkpoint.shape
    tops = expert_ids.shape[1]

    def over_x(value):
        return lax.ppermute(value, "tensor", [(0, 1), (1, 0)])

    def over_core(value):
        return lax.ppermute(value, "dp", [(0, 1), (1, 0)])

    def over_y(value):
        return lax.ppermute(value, "expert", [(e, e ^ 1) for e in range(experts)])

    order = [*range(0, ring, 2)][:1] + [*range(1, ring, 2)] + [*range(2, ring, 2)][::-1]
    spot = {slow: at for at, slow in enumerate(order)}

    def moved(e, shift):
        return order[(spot[e // 2] + shift) % ring] * 2 + e % 2

    def over_z(value, shift):
        return lax.ppermute(value, "expert", [(e, moved(e, shift)) for e in range(experts)])

    def after(values, *earlier):
        return lax.optimization_barrier((values, earlier))[0]

    pick_rows = -(-3 * tops * token_rows // (16 * width)) * 16
    x_count, g_count = 2 * token_rows + pick_rows, 2 * token_rows

    info = jnp.stack([side, core * experts + place, (1 - core) * experts + place])
    mine = sum(jnp.where(place // 2 == slow, at, 0) for at, slow in enumerate(order))
    owners = []
    for step in range(ring):
        spot_there = (mine + step) % ring
        there = sum(jnp.where(spot_there == at, slow, 0) for at, slow in enumerate(order))
        for way in range(2):
            for which in range(2):
                owners.append((core ^ which) * experts + there * 2 + (place % 2 ^ way))
    owners = jnp.stack(owners)
    checkpoint, out_grad, w_gate, w_up, w_down = after((checkpoint, out_grad, w_gate, w_up, w_down), info, owners)

    x = (checkpoint.astype(jnp.float32) * scales[:, None]).astype(jnp.bfloat16)
    x = lax.optimization_barrier(x)
    near, x_other = (over_z(x, 1), over_z(out_grad, 1)), over_x(x)
    others = [over_core(w[0]) for w in after((w_gate, w_up, w_down), x)]
    g_other = over_y(after(out_grad, others[0]))
    ids_t, gates_t = after((expert_ids.T, gates.T), others[0])
    (picks,) = move_rows(picks_kernel, (pick_rows,), width, ids_t, gates_t)
    picks, x_other = lax.optimization_barrier((picks, x_other))
    (both,) = move_rows(stack_kernel, (x_count,), width, x_other, g_other, picks)
    both_near = over_z(both, 1)
    near = after(near, both)
    terms, shares, tokens, hops, outs = [[None] * ring for _ in range(5)]

    def hop(step):
        xs, gs = shares[step]
        tokens[step] = over_y(xs), over_x(gs)

    shares[0] = move_rows(merge_kernel, (x_count, g_count), width, x, out_grad, both)
    hop(0)
    others = after(others, near)
    wg, wu, wd = [jnp.concatenate([w[0], far], axis=0) for w, far in zip((w_gate, w_up, w_down), others)]
    near, both_near, wg, wu, wd = lax.optimization_barrier((near, both_near, wg, wu, wd))
    um, *shares[1] = move_rows(join_kernel, (x_count + g_count, x_count, g_count), width, *near, both_near)

    def expert(step):
        *outs, term = run_expert(tops, token_rows, info, *shares[step], *tokens[step], wg, wu, wd)
        terms[step] = term[:, 0]
        return outs

    def kernel_and_hop(step):
        outs[step] = expert(step)
        hops[step] = over_x(outs[step][0]), over_y(outs[step][2])

    moving = None
    for step in range(1, ring):
        if step > 1:
            shares[step] = move_rows(split_kernel, (x_count, g_count), width, um)
        hop(step)
        if step < ring - 1:
            following = over_z(um, 1)
        if step == 1:
            tokens[0] = after(tokens[0], um, shares[1])
            kernel_and_hop(0)
        if step > 1:
            hops[step - 1] = after(hops[step - 1], tokens[step])
        if step == ring - 1:
            for back in range(1, ring - 1):
                more_a, more_b = ((), ()) if moving is None else ((moving[:2],), (moving[2:],))
                (_, a_keep, _, b_keep), (a_got, b_got) = outs[back], hops[back]
                late = jnp.concatenate([add(a_keep, a_got, *more_a), add(b_keep, b_got, *more_b)])
                late = lax.optimization_barrier(after(late, shares[step]))
                moving = over_z(late, 1)
            tokens[step] = after(tokens[step], late)
        kernel_and_hop(step)
        if step < ring - 1:
            um = after(following, outs[step - 1], hops[step - 1])
    (_, a_keep, _, b_keep), (a_got, b_got) = outs[-1], hops[-1]
    term = jnp.stack(terms).reshape(ring, 2, 2, token_rows)
    term_far = over_x(term)
    a_got, b_got = after((a_got, b_got), term_far)
    a_next, b_next = add(a_keep[1], a_got[1], moving[1]), add(b_keep[1], b_got[1], moving[3])
    term = after(term + term_far, a_next, b_next)
    term = [term[step] if step == 0 else over_z(term[step], -step) for step in range(ring)]
    a = add(a_keep[0], a_got[0], moving[0], over_y(a_next))
    b = add(b_keep[0], b_got[0], moving[2], over_x(b_next))
    last = lax.optimization_barrier(jnp.concatenate([a, b]))
    moving = over_z(last, 1)
    (_, a_keep, _, b_keep), (a_got, b_got) = outs[0], after(hops[0], last)
    a0_next, b0_next = add(a_keep[1], a_got[1]), add(b_keep[1], b_got[1])
    a0, b0 = add(a_keep[0], a_got[0], over_y(a0_next)), add(b_keep[0], b_got[0], over_x(b0_next))
    term = jnp.stack(after(term, a0_next, b0_next))
    term = term[:, :, 0], over_y(term[:, :, 1])
    half = token_rows // 2
    total = jnp.concatenate([add(a0, moving[:half]), add(b0, moving[half:])])
    vmem = pl.BlockSpec(memory_space=pltpu.VMEM)
    gate_out = pl.pallas_call(
        pick_kernel,
        in_specs=[pl.BlockSpec(memory_space=pltpu.SMEM)] + [vmem] * (1 + len(term)),
        out_specs=vmem,
        out_shape=jax.ShapeDtypeStruct((tops, token_rows), jnp.float32),
        compiler_params=pltpu.CompilerParams(vmem_limit_bytes=4 * 1024 * 1024),
    )(owners, expert_ids.T, *term).T
    return (total, gate_out)


def body(checkpoint, scales, out_grad, expert_ids, gates, w_gate, w_up, w_down):
    experts = lax.axis_size("expert")
    token_rows, width = checkpoint.shape
    pairs = lax.axis_size("dp") == 2 and lax.axis_size("tensor") == 2 and experts % 2 == 0
    fits = token_rows % 128 == 0 and width % token_rows == 0
    dense = pairs and fits and expert_ids.shape[1] >= experts > 4
    chosen = body_dense if dense else body_routed
    return chosen(checkpoint, scales, out_grad, expert_ids, gates, w_gate, w_up, w_down)


def solution(mesh):
    return jax.shard_map(
        body,
        mesh=mesh,
        in_specs=(
            P(("dp", "expert"), "tensor"),
            P(("dp", "expert")),
            P(("dp", "expert"), "tensor"),
            P(("dp", "expert"), None),
            P(("dp", "expert"), None),
            P(("dp", "expert"), "tensor", None),
            P(("dp", "expert"), "tensor", None),
            P(("dp", "expert"), "tensor", None),
        ),
        out_specs=(P(("dp", "expert"), "tensor"), P(("dp", "expert"), None)),
        check_vma=False,
    )
```

```python
import functools
import jax
import jax.numpy as jnp
from jax import lax
from jax.experimental import pallas as pl
from jax.experimental.pallas import tpu as pltpu
from jax.sharding import PartitionSpec as P


def slot_table(expert_ids, expert_count, slot_cap):
    token_rows = expert_ids.shape[0]
    pick_count = expert_ids.shape[1]
    chosen = expert_ids.reshape(-1)
    onehot = (chosen[:, None] == jnp.arange(expert_count, dtype=jnp.int32)[None, :]).astype(
        jnp.int32
    )
    earlier = jnp.cumsum(onehot, axis=0) - onehot
    position = jnp.sum(earlier * onehot, axis=1)
    slot_of = chosen * slot_cap + position
    token_ids = jnp.arange(token_rows * pick_count, dtype=jnp.int32) // pick_count
    owner = jnp.full((expert_count * slot_cap,), token_rows, jnp.int32).at[slot_of].set(token_ids)
    return (slot_of, owner)


def finish(gate_pre, up_pre, back, weight_gate, weight_up):
    sigma = jax.nn.sigmoid(gate_pre)
    swish = gate_pre * sigma
    hidden = (swish * up_pre).astype(jnp.bfloat16)
    gate_part = jnp.sum(hidden.astype(jnp.float32) * back, axis=1).astype(jnp.bfloat16)
    d_gate = (back * up_pre * sigma * (1.0 + gate_pre * (1.0 - sigma))).astype(jnp.bfloat16)
    d_up = (back * swish).astype(jnp.bfloat16)
    input_part = jnp.dot(d_gate, weight_gate, preferred_element_type=jnp.float32)
    input_part = input_part + jnp.dot(d_up, weight_up, preferred_element_type=jnp.float32)
    return (input_part.astype(jnp.bfloat16), gate_part)


def close_expert(input_part, gate_part, sources, items, model_width):
    shaped = input_part.reshape(sources, items, model_width)
    gate_shaped = gate_part.reshape(sources, items)
    summed = lax.psum_scatter(
        shaped.astype(jnp.float32).astype(jnp.bfloat16), "tensor", scatter_dimension=2, tiled=True
    )
    return (summed, gate_shaped)


def body_routed(checkpoint, scales, out_grad, expert_ids, gates, w_gate, w_up, w_down):
    expert_count = lax.axis_size("dp") * lax.axis_size("expert")
    token_rows = checkpoint.shape[0]
    pick_count = expert_ids.shape[1]
    slot_cap = min(token_rows, token_rows * pick_count // expert_count)
    weight_gate = w_gate[0]
    weight_up = w_up[0]
    weight_down = w_down[0]
    model_width = weight_gate.shape[1]
    contract = (((1,), (1,)), ((), ()))
    dequant = (checkpoint.astype(jnp.float32) * scales[:, None]).astype(jnp.bfloat16)
    slot_of, owner = slot_table(expert_ids, expert_count, slot_cap)
    full_x, full_grad = (
        lax.all_gather(dequant, "tensor", axis=1, tiled=True),
        lax.all_gather(out_grad, "tensor", axis=1, tiled=True),
    )
    send_x = jnp.take(full_x, owner, axis=0, mode="fill", fill_value=0).reshape(
        expert_count, slot_cap, model_width
    )
    send_grad = jnp.take(full_grad, owner, axis=0, mode="fill", fill_value=0).reshape(
        expert_count, slot_cap, model_width
    )
    rows_in = lax.all_to_all(send_x, ("dp", "expert"), split_axis=0, concat_axis=0, tiled=True)
    grads_in = lax.all_to_all(send_grad, ("dp", "expert"), split_axis=0, concat_axis=0, tiled=True)
    sources, items, width = rows_in.shape
    rows_flat = rows_in.reshape(sources * items, width)
    grads_flat = grads_in.reshape(sources * items, width)
    gate_pre = lax.dot_general(rows_flat, weight_gate, contract, preferred_element_type=jnp.float32)
    up_pre = lax.dot_general(rows_flat, weight_up, contract, preferred_element_type=jnp.float32)
    back = lax.dot_general(grads_flat, weight_down, contract, preferred_element_type=jnp.float32)
    input_part, gate_part = finish(gate_pre, up_pre, back, weight_gate, weight_up)
    input_part, gate_part = close_expert(input_part, gate_part, sources, items, model_width)
    back_input, back_gate = (
        lax.all_to_all(input_part, ("dp", "expert"), split_axis=0, concat_axis=0, tiled=True),
        lax.all_to_all(gate_part, ("dp", "expert"), split_axis=0, concat_axis=0, tiled=True),
    )
    share_width = back_input.shape[2]
    picked = jnp.take(back_input.reshape(expert_count * slot_cap, share_width), slot_of, axis=0)
    picked = picked.astype(jnp.float32).reshape(token_rows, pick_count, share_width)
    weighted = jnp.sum(picked * gates[:, :, None], axis=1)
    gate_pairs = (
        jnp.take(back_gate.reshape(-1), slot_of, axis=0)
        .astype(jnp.float32)
        .reshape(token_rows, pick_count)
    )
    gate_out = lax.psum(gate_pairs.astype(jnp.bfloat16), "tensor").astype(jnp.float32)
    return (weighted.astype(jnp.bfloat16), gate_out)


def expert_kernel(tops, info_ref, xs_ref, gs_ref, v_ref, n_ref, wg_ref, wu_ref, wd_ref, *outs):
    a_send, a_keep, b_send, b_keep, term_ref = outs
    f32 = jnp.float32
    contract = (((1,), (1,)), ((), ()))
    _, half, width = a_send.shape
    token_rows = 2 * half
    rows = 2 * token_rows
    units = wg_ref.shape[0] // 2
    mine = pl.ds(pl.multiple_of(info_ref[0] * width, width), width)
    other = pl.ds(pl.multiple_of((1 - info_ref[0]) * width, width), width)

    def project(first, second, w_ref):
        low = lax.dot_general(first, w_ref[:, mine], contract, preferred_element_type=f32)
        return low + lax.dot_general(second, w_ref[:, other], contract, preferred_element_type=f32)

    def weight_of(pick_rows, expert):

        def segment(kind, k):
            at = (kind * tops + k) * token_rows
            row, col = at // width, at % width
            return pick_rows[row : row + 1, col : col + token_rows].astype(f32)

        total = jnp.zeros((1, token_rows), f32)
        for k in range(tops):
            chosen = segment(0, k) == expert.astype(f32)
            total = total + jnp.where(chosen, segment(1, k) + segment(2, k), 0.0)
        return jnp.broadcast_to(total, (128, token_rows)).T[:, :1]

    x_mine = jnp.concatenate([xs_ref[token_rows:rows], v_ref[token_rows:rows]], axis=0)
    x_other = jnp.concatenate([xs_ref[:token_rows], v_ref[:token_rows]], axis=0)
    picks = xs_ref[rows:], v_ref[rows:]
    gate_pre = project(x_mine, x_other, wg_ref)
    up_pre = project(x_mine, x_other, wu_ref)
    back = project(gs_ref[...], n_ref[...], wd_ref)
    sigma = jax.nn.sigmoid(gate_pre)
    swish = gate_pre * sigma
    hidden = (swish * up_pre).astype(jnp.bfloat16)
    product = hidden.astype(f32) * back
    weights = []
    for which in range(2):
        expert = info_ref[1 + which]
        weights.append(jnp.concatenate([weight_of(part, expert) for part in picks], axis=0))
        term = jnp.sum(product[:, which * units : (which + 1) * units], axis=1, keepdims=True)
        term = term.astype(jnp.bfloat16).astype(f32)
        term_ref[which] = jnp.broadcast_to(term, (rows, 128)).T[:8]
    lane = lax.broadcasted_iota(jnp.int32, back.shape, 1)
    scaled = back * jnp.where(lane < units, weights[0], weights[1])
    d_gate = (scaled * up_pre * sigma * (1.0 + gate_pre * (1.0 - sigma))).astype(jnp.bfloat16)
    d_up = (scaled * swish).astype(jnp.bfloat16)

    def spread(cols):
        piece = jnp.dot(d_gate, wg_ref[:, cols], preferred_element_type=f32)
        piece = piece + jnp.dot(d_up, wu_ref[:, cols], preferred_element_type=f32)
        return piece.astype(jnp.bfloat16)

    far, near = spread(other), spread(mine)
    a_send[0], a_send[1] = far[:half], far[token_rows : token_rows + half]
    b_keep[1], b_send[1] = far[half:token_rows], far[token_rows + half :]
    a_keep[0], a_keep[1] = near[:half], near[token_rows : token_rows + half]
    b_keep[0], b_send[0] = near[half:token_rows], near[token_rows + half :]


def run_expert(tops, token_rows, info, xs, gs, v, n, wg, wu, wd):
    hidden, model_width = wg.shape
    rows = 2 * token_rows
    vmem = pl.BlockSpec(memory_space=pltpu.VMEM)
    share = jax.ShapeDtypeStruct((2, token_rows // 2, xs.shape[1]), jnp.bfloat16)
    return pl.pallas_call(
        functools.partial(expert_kernel, tops),
        in_specs=[pl.BlockSpec(memory_space=pltpu.SMEM)] + [vmem] * 7,
        out_specs=[vmem] * 5,
        out_shape=[share] * 4 + [jax.ShapeDtypeStruct((2, 8, rows), jnp.float32)],
        compiler_params=pltpu.CompilerParams(vmem_limit_bytes=16 * 1024 * 1024),
        cost_estimate=pl.CostEstimate(
            flops=10 * rows * hidden * model_width,
            bytes_accessed=6 * rows * model_width + 6 * hidden * model_width,
            transcendentals=rows * hidden,
        ),
    )(info, xs, gs, v, n, wg, wu, wd)


def stack_kernel(x_far, g_far, ids, gates, both):
    f32 = jnp.float32
    token_rows, width = x_far.shape
    both[:token_rows] = x_far[...]
    both[token_rows : 2 * token_rows] = g_far[...]
    high = gates[...].astype(jnp.bfloat16).astype(f32)
    parts = [ids[...].astype(f32), high, gates[...] - high]
    flat = [part[k : k + 1] for part in parts for k in range(part.shape[0])]
    count = both.shape[0] - 2 * token_rows
    flat += [jnp.zeros((1, token_rows), f32)] * (count * width // token_rows - len(flat))
    per = width // token_rows
    rows = [jnp.concatenate(flat[row * per : (row + 1) * per], axis=1) for row in range(count)]
    both[2 * token_rows :] = jnp.concatenate(rows, axis=0).astype(jnp.bfloat16)


def merge_kernel(own, both, xs, gs):
    token_rows = own.shape[0] // 2
    xs[:token_rows] = both[:token_rows]
    xs[token_rows : 2 * token_rows] = own[:token_rows]
    xs[2 * token_rows :] = both[2 * token_rows :]
    gs[:token_rows] = own[token_rows:]
    gs[token_rows:] = both[token_rows : 2 * token_rows]


def join_kernel(own, both, um, xs, gs):
    merge_kernel(own, both, xs, gs)
    split = xs.shape[0]
    merge_kernel(own, both, um.at[:split], um.at[split:])


def pick_kernel(owners, ids, *refs):
    terms, out = refs[:-1], refs[-1]
    total = jnp.zeros(out.shape, jnp.float32)
    for way, ref in enumerate(terms):
        steps, which_count, _ = ref.shape
        for step in range(steps):
            for which in range(which_count):
                owner = owners[(step * len(terms) + way) * which_count + which]
                total = total + jnp.where(ids[...] == owner, ref[step, which : which + 1], 0.0)
    out[...] = total


def split_kernel(um, xs, gs):
    xs[...] = um[: xs.shape[0]]
    gs[...] = um[xs.shape[0] :]


def move_rows(kernel, rows, *values):
    vmem = pl.BlockSpec(memory_space=pltpu.VMEM)
    width = values[0].shape[1]
    return pl.pallas_call(
        kernel,
        in_specs=[vmem] * len(values),
        out_specs=[vmem] * len(rows),
        out_shape=[jax.ShapeDtypeStruct((count, width), jnp.bfloat16) for count in rows],
        compiler_params=pltpu.CompilerParams(vmem_limit_bytes=4 * 1024 * 1024),
        cost_estimate=pl.CostEstimate(flops=0, bytes_accessed=4 * sum(rows) * width, transcendentals=0),
    )(*values)


def add(*values):
    return sum(value.astype(jnp.float32) for value in values).astype(jnp.bfloat16)


def body_dense(checkpoint, scales, out_grad, expert_ids, gates, w_gate, w_up, w_down):
    experts = lax.axis_size("expert")
    ring = experts // 2
    core = lax.axis_index("dp")
    place = lax.axis_index("expert")
    side = lax.axis_index("tensor")
    token_rows, width = checkpoint.shape
    tops = expert_ids.shape[1]

    def over_x(value):
        return lax.ppermute(value, "tensor", [(0, 1), (1, 0)])

    def over_core(value):
        return lax.ppermute(value, "dp", [(0, 1), (1, 0)])

    def over_y(value):
        return lax.ppermute(value, "expert", [(e, e ^ 1) for e in range(experts)])

    order = [*range(0, ring, 2)][:1] + [*range(1, ring, 2)] + [*range(2, ring, 2)][::-1]
    spot = {slow: at for at, slow in enumerate(order)}

    def moved(e, shift):
        return order[(spot[e // 2] + shift) % ring] * 2 + e % 2

    def over_z(value, shift):
        return lax.ppermute(value, "expert", [(e, moved(e, shift)) for e in range(experts)])

    def after(values, *earlier):
        return lax.optimization_barrier((values, earlier))[0]

    pick_rows = -(-3 * tops * token_rows // (16 * width)) * 16
    x_count, g_count = 2 * token_rows + pick_rows, 2 * token_rows

    info = jnp.stack([side, core * experts + place, (1 - core) * experts + place])
    mine = sum(jnp.where(place // 2 == slow, at, 0) for at, slow in enumerate(order))
    owners = []
    for step in range(ring):
        spot_there = (mine + step) % ring
        there = sum(jnp.where(spot_there == at, slow, 0) for at, slow in enumerate(order))
        for way in range(2):
            for which in range(2):
                owners.append((core ^ which) * experts + there * 2 + (place % 2 ^ way))
    owners = jnp.stack(owners)
    checkpoint, out_grad, w_gate, w_up, w_down = after((checkpoint, out_grad, w_gate, w_up, w_down), info, owners)

    x = (checkpoint.astype(jnp.float32) * scales[:, None]).astype(jnp.bfloat16)
    own = lax.optimization_barrier(jnp.concatenate([x, out_grad]))
    near, x_other = over_z(own, 1), over_x(x)
    others = [over_core(w[0]) for w in after((w_gate, w_up, w_down), own)]
    g_other = over_y(after(out_grad, others[0]))
    ids_t, gates_t = after((expert_ids.T, gates.T), x_other)
    (both,) = move_rows(stack_kernel, (x_count,), x_other, g_other, ids_t, gates_t)
    both_near = over_z(both, 1)
    near = after(near, both)
    terms, shares, tokens, hops, outs = [[None] * ring for _ in range(5)]

    def hop(step):
        xs, gs = shares[step]
        tokens[step] = over_y(xs), over_x(gs)

    shares[0] = move_rows(merge_kernel, (x_count, g_count), own, both)
    hop(0)
    others = after(others, near)
    wg, wu, wd = [jnp.concatenate([w[0], far], axis=0) for w, far in zip((w_gate, w_up, w_down), others)]
    near, both_near, wg, wu, wd = lax.optimization_barrier((near, both_near, wg, wu, wd))
    um, *shares[1] = move_rows(join_kernel, (x_count + g_count, x_count, g_count), near, both_near)

    def expert(step):
        *outs, term = run_expert(tops, token_rows, info, *shares[step], *tokens[step], wg, wu, wd)
        terms[step] = term[:, 0]
        return outs

    def kernel_and_hop(step):
        outs[step] = expert(step)
        hops[step] = over_x(outs[step][0]), over_y(outs[step][2])

    moving = None
    for step in range(1, ring):
        if step > 1:
            shares[step] = move_rows(split_kernel, (x_count, g_count), um)
        hop(step)
        if step < ring - 1:
            following = over_z(um, 1)
        if step == 1:
            tokens[0] = after(tokens[0], um, shares[1])
            kernel_and_hop(0)
        if step > 1:
            hops[step - 1] = after(hops[step - 1], tokens[step])
        if step == ring - 1:
            for back in range(1, ring - 1):
                more_a, more_b = ((), ()) if moving is None else ((moving[:2],), (moving[2:],))
                (_, a_keep, _, b_keep), (a_got, b_got) = outs[back], hops[back]
                late = jnp.concatenate([add(a_keep, a_got, *more_a), add(b_keep, b_got, *more_b)])
                late = lax.optimization_barrier(after(late, shares[step]))
                moving = over_z(late, 1)
            tokens[step] = after(tokens[step], late)
        kernel_and_hop(step)
        if step < ring - 1:
            um = after(following, outs[step - 1], hops[step - 1])
    (_, a_keep, _, b_keep), (a_got, b_got) = outs[-1], hops[-1]
    term = jnp.stack(terms).reshape(ring, 2, 2, token_rows)
    term_far = over_x(term)
    b_got = after(b_got, term_far)
    a_next, b_next = add(a_keep[1], a_got[1], moving[1]), add(b_keep[1], b_got[1], moving[3])
    term = after(term + term_far, a_next, b_next)
    term = [term[step] if step == 0 else over_z(term[step], -step) for step in range(ring)]
    a = add(a_keep[0], a_got[0], moving[0], after(over_y(a_next), b_next))
    b = add(b_keep[0], b_got[0], moving[2], over_x(b_next))
    last = lax.optimization_barrier(jnp.concatenate([a, b]))
    moving = over_z(last, 1)
    (_, a_keep, _, b_keep), (a_got, b_got) = outs[0], after(hops[0], last)
    a0_next, b0_next = add(a_keep[1], a_got[1]), add(b_keep[1], b_got[1])
    a0, b0 = add(a_keep[0], a_got[0], over_y(a0_next)), add(b_keep[0], b_got[0], over_x(b0_next))
    term = jnp.stack(after(term, a0_next, b0_next))
    term = term[:, :, 0], over_y(term[:, :, 1])
    half = token_rows // 2
    total = jnp.concatenate([add(a0, moving[:half]), add(b0, moving[half:])])
    vmem = pl.BlockSpec(memory_space=pltpu.VMEM)
    gate_out = pl.pallas_call(
        pick_kernel,
        in_specs=[pl.BlockSpec(memory_space=pltpu.SMEM)] + [vmem] * (1 + len(term)),
        out_specs=vmem,
        out_shape=jax.ShapeDtypeStruct((tops, token_rows), jnp.float32),
        compiler_params=pltpu.CompilerParams(vmem_limit_bytes=4 * 1024 * 1024),
    )(owners, expert_ids.T, *term).T
    return (total, gate_out)


def body(checkpoint, scales, out_grad, expert_ids, gates, w_gate, w_up, w_down):
    experts = lax.axis_size("expert")
    token_rows, width = checkpoint.shape
    pairs = lax.axis_size("dp") == 2 and lax.axis_size("tensor") == 2 and experts % 2 == 0
    fits = token_rows % 128 == 0 and width % token_rows == 0
    dense = pairs and fits and expert_ids.shape[1] >= experts > 4
    chosen = body_dense if dense else body_routed
    return chosen(checkpoint, scales, out_grad, expert_ids, gates, w_gate, w_up, w_down)


def solution(mesh):
    return jax.shard_map(
        body,
        mesh=mesh,
        in_specs=(
            P(("dp", "expert"), "tensor"),
            P(("dp", "expert")),
            P(("dp", "expert"), "tensor"),
            P(("dp", "expert"), None),
            P(("dp", "expert"), None),
            P(("dp", "expert"), "tensor", None),
            P(("dp", "expert"), "tensor", None),
            P(("dp", "expert"), "tensor", None),
        ),
        out_specs=(P(("dp", "expert"), "tensor"), P(("dp", "expert"), None)),
        check_vma=False,
    )
```
